32 devices in a mesh: parts: 2 (over y), row: 4 (over z), col: 2 (over x), sub: 2 (over core).
Axes of the slice: x: 2, y: 2, z: 4, core: 2. Of those that a mesh axis runs over, the one named last changes fastest.
Arguments:
- ancestor_cov: float32 [64, 32, 256, 256], P(('parts', 'row'), 'col'), parts along dimension 0, may hold values from -6 to 6
- owner_slot: int32 [64], P('parts'), parts along dimension 0, may hold values from 0 to 31, each once
- parent_pattern: int32 [8, 12], P(('parts', 'sub')), parts along dimension 0, may hold values from 0 to 31, as said below
- parent_factor: float32 [8, 12, 256, 256], P(('parts', 'sub'), None, 'row'), parts along dimension 0, may hold values from -0.109375 to 0.109375
- parent_inverse: float32 [8, 256, 256], P(('parts', 'sub')), parts along dimension 0, may hold values from -6 to 6
- child_parent: int32 [8], P(('parts', 'sub')), parts along dimension 0, may hold values from 0 to 1
- child_pattern: int32 [8, 8], P(('parts', 'sub')), parts along dimension 0, may hold values from 0 to 11, as said below
- child_factor: float32 [8, 9, 256, 256], P(('parts', 'sub'), None, 'row'), parts along dimension 0, may hold values from -0.125 to 0.125
- child_inverse: float32 [8, 256, 256], P(('parts', 'sub')), parts along dimension 0, may hold values from -6 to 6
Outputs:
- parent_cov: float32 [8, 32, 256, 256], P(('parts', 'sub'), 'row'), parts along dimension 0
- parent_diag: float32 [8, 256, 256], P(('parts', 'sub')), parts along dimension 0
- child_cov: float32 [8, 32, 256, 256], P(('parts', 'sub'), 'row'), parts along dimension 0
- child_upper: float32 [8, 256, 256], P(('parts', 'sub')), parts along dimension 0
- child_diag: float32 [8, 256, 256], P(('parts', 'sub')), parts along dimension 0
The draws below stay inside these ranges and needn't reach their ends.
There are 2 independent parts, one for each index of `parts`. The reference program is written for one: setup_inputs(seed, part) draws one part's arguments, and reference() takes and returns one part's arrays. A program takes and returns all parts, laid end to end along the dimension named above; each array names one. Nothing has to cross between parts.
Inputs may be any that keep to these rules, and one draw needn't show every extreme that they name: `parent_pattern`: each row holds distinct ancestor ids. `child_pattern`: each row holds distinct positions.
All inputs are finite; a program needn't handle non-finite values.
Results may differ from the reference program's by a relative error of at most 0.0001.
Values sent between devices are 32-bit elements; how exact they have to be, the bound alone decides.
No kernel may reach another device: no remote copies, remote signals or barrier semaphores. Data moves between devices by JAX's collectives and lax.ppermute only.
A program may use at most 192 MiB of HBM per device.

```python
import jax
import jax.numpy as jnp
from jax import lax

BLOCK = 256
ANCESTORS = 32
PARENT_ROWS = 12
CHILD_ROWS = 8
GROUP_PARENTS = 2
PARENTS = 4
CHILDREN = 4


def draw_parent_pattern(key, part):
    keys = jax.random.split(jax.random.fold_in(key, 11), PARENTS)
    rows = jax.vmap(lambda one: jax.random.permutation(one, ANCESTORS)[:PARENT_ROWS])(keys)
    return rows.astype(jnp.int32)


def draw_child_pattern(key, part):
    keys = jax.random.split(jax.random.fold_in(key, 23), CHILDREN)
    rows = jax.vmap(lambda one: jax.random.permutation(one, PARENT_ROWS)[:CHILD_ROWS])(keys)
    return rows.astype(jnp.int32)


def place_ends(array, own_key, low, largest):
    shape = array.shape
    index_at = [jax.random.randint(jax.random.fold_in(own_key, axis), (), 0, shape[axis]) for axis in range(len(shape))]
    array = array.at[tuple(index_at)].set(low)
    longest = shape.index(max(shape))
    index_at[longest] = (index_at[longest] + 1) % shape[longest]
    return array.at[tuple(index_at)].set(largest)


def block_scale(key, extent, cuts, smallest, largest):
    level = 1.0
    for dim, blocks in cuts:
        steps = jax.random.uniform(jax.random.fold_in(jax.random.fold_in(key, 6), dim), (blocks,), jnp.float32, smallest / len(cuts), largest / len(cuts))
        level = level * jnp.repeat(jnp.exp(steps), extent[dim] // blocks).reshape((-1,) + (1,) * (len(extent) - 1 - dim))
    return level


def noise(rng, shape, deviation, bound, shards=(), kind=jnp.bfloat16):
    array = jax.random.normal(rng, shape, jnp.float32) * deviation
    if len(shards) > 0:
        array = block_scale(rng, shape, shards, -0.22, 0.18) * array
    return jnp.clip(array, min=-bound, max=bound).astype(kind)


def setup_inputs(seed: int = 0, part: int = 0) -> dict:
    key_list = jax.random.split(jax.random.key(seed), 10)
    part_splits = jax.random.split(jax.random.fold_in(key_list[9], part), 10)
    ancestor_cov = noise(part_splits[0], (ANCESTORS, ANCESTORS, BLOCK, BLOCK), 1.0, 6.0, ((0, 4), (1, 2)), jnp.float32)
    owner_slot = jax.random.permutation(part_splits[1], ANCESTORS).astype(jnp.int32)
    parent_pattern = draw_parent_pattern(jax.random.fold_in(jax.random.fold_in(key_list[9], part), 71), part)
    parent_factor = noise(part_splits[3], (PARENTS, PARENT_ROWS, BLOCK, BLOCK), (PARENT_ROWS * BLOCK) ** -0.5, 0.109375, ((0, 2), (2, 4)), jnp.float32)
    parent_inverse = noise(part_splits[4], (PARENTS, BLOCK, BLOCK), 1.0, 6.0, ((0, 2),), jnp.float32)
    child_parent = place_ends(jax.random.randint(part_splits[5], (CHILDREN,), 0, GROUP_PARENTS), jax.random.fold_in(part_splits[5], 1), 0, GROUP_PARENTS - 1).astype(jnp.int32)
    child_pattern = draw_child_pattern(jax.random.fold_in(jax.random.fold_in(key_list[9], part), 71), part)
    child_factor = noise(part_splits[7], (CHILDREN, CHILD_ROWS + 1, BLOCK, BLOCK), ((CHILD_ROWS + 1) * BLOCK) ** -0.5, 0.125, ((0, 2), (2, 4)), jnp.float32)
    child_inverse = noise(part_splits[8], (CHILDREN, BLOCK, BLOCK), 1.0, 6.0, ((0, 2),), jnp.float32)
    return dict(ancestor_cov=ancestor_cov, owner_slot=owner_slot, parent_pattern=parent_pattern, parent_factor=parent_factor, parent_inverse=parent_inverse, child_parent=child_parent, child_pattern=child_pattern, child_factor=child_factor, child_inverse=child_inverse)


HIGH = lax.Precision.HIGHEST


def dense_blocks(slot_list, blocks):
    onehot = (slot_list[:, None] == jnp.arange(ANCESTORS, dtype=jnp.int32)[None, :]).astype(jnp.float32)
    placed = jnp.einsum('ps,pxy->sxy', onehot, blocks.astype(jnp.float32), precision=HIGH)
    return placed, jnp.sum(onehot, axis=0)


def reference(ancestor_cov, owner_slot, parent_pattern, parent_factor, parent_inverse, child_parent, child_pattern, child_factor, child_inverse):
    ancestor_ids = jnp.arange(ANCESTORS, dtype=jnp.int32)
    match = (parent_pattern[:, :, None] == ancestor_ids[None, None, :]).astype(jnp.int32)
    slots = jnp.sum(match * owner_slot[None, None, :], axis=-1).astype(jnp.int32)
    cov_list = []
    diag_list = []
    for j in range(PARENTS):
        placed, mask = dense_blocks(slots[j], parent_factor[j])
        prod = jnp.einsum('stxy,tyz->sxz', ancestor_cov, placed, precision=HIGH)
        cov = -mask[:, None, None] * prod
        diag = parent_inverse[j] + jnp.einsum('sxy,sxz->yz', placed, cov, precision=HIGH)
        cov_list.append(cov)
        diag_list.append(diag)
    parent_cov = jnp.stack(cov_list)
    parent_diag = jnp.stack(diag_list)
    kid_cov = []
    kid_upper = []
    kid_diag = []
    for k in range(CHILDREN):
        parent = ((k // GROUP_PARENTS) * GROUP_PARENTS + child_parent[k]).astype(jnp.int32)
        parent_slots = jnp.take(slots, parent, axis=0)
        kid_slots = jnp.take(parent_slots, child_pattern[k].astype(jnp.int32), axis=0)
        placed, mask = dense_blocks(kid_slots, child_factor[k, 1:])
        lead = child_factor[k, 0]
        pcov = jnp.take(parent_cov, parent, axis=0)
        pdiag = jnp.take(parent_diag, parent, axis=0)
        prod = jnp.einsum('stxy,tyz->sxz', ancestor_cov, placed, precision=HIGH)
        prod = prod + jnp.einsum('sxy,yz->sxz', pcov, lead, precision=HIGH)
        kid_cov.append(-mask[:, None, None] * prod)
        upper = jnp.dot(pdiag, lead, precision=HIGH) + jnp.einsum('sxy,sxz->yz', pcov, placed, precision=HIGH)
        kid_upper.append(-upper)
        diag = child_inverse[k] - jnp.dot(lead.T, upper, precision=HIGH) - jnp.einsum('sxy,sxz->yz', placed, prod, precision=HIGH)
        kid_diag.append(diag)
    return (parent_cov, parent_diag, jnp.stack(kid_cov), jnp.stack(kid_upper), jnp.stack(kid_diag))
```

```python
import functools

import jax
import jax.numpy as jnp
from jax import lax
from jax.experimental import pallas as pl
from jax.experimental.pallas import tpu as pltpu
from jax.sharding import PartitionSpec as P

HIGH = lax.Precision.HIGHEST
VMEM_LIMIT = 50 * 1024 * 1024
SLACK = 4
DEPTH = 8
SMEM = pl.BlockSpec(memory_space=pltpu.SMEM)
VMEM = pl.BlockSpec(memory_space=pltpu.VMEM)
HBM = pl.BlockSpec(memory_space=pl.ANY)


class Layout:
    def __init__(self, count, length, lead, row_slots, col_slots, rows, cols):
        self.count, self.length, self.lead = count, length, lead
        self.row_slots, self.col_slots, self.rows, self.cols = row_slots, col_slots, rows, cols
        total = count * length
        self.full_w = total + lead
        self.cap_w = min(total, -(-total // cols) + SLACK) + lead
        self.full_y = count * min(length, row_slots)
        self.cap_y = min(self.full_y, -(-total // rows) + SLACK)
        products = self.full_y * min(length, col_slots)
        self.y_at = 4
        self.out_at = self.y_at + 4 * self.full_y
        self.a_at = self.out_at + count * row_slots
        self.w_at = self.a_at + products
        self.p_at = self.w_at + products
        self.size = self.p_at + products


def plan_kernel(lay, upper, here, owner, parents, kid_parent, kid_pattern, factor, tab, most, send, spill, *scratch):
    col_count, row_count, at_block, sems = scratch
    row, col = here[0], here[1]
    held = send.shape[0]
    for i in range(lay.cols):
        col_count[i] = 0
    for i in range(lay.rows):
        row_count[i] = 0

    def clear(i, _):
        tab[lay.out_at + i] = -1
        return 0

    lax.fori_loop(0, lay.count * lay.row_slots, clear, 0)

    def copy_to(target, source, place):
        return pltpu.make_async_copy(factor.at[source // (lay.length + upper_lead), source % (lay.length + upper_lead)], target, sems.at[place])

    upper_lead = 1 if lay.lead else 0
    for m in range(lay.lead):
        copy_to(send.at[m], m * (lay.length + 1), m).start()
    blocks, listed, products = jnp.int32(lay.lead), jnp.int32(0), jnp.int32(0)
    for m in range(lay.count):
        first_block, first_row = blocks, listed
        parent = m if upper else kid_parent[m]

        def visit(p, carry):
            blocks, listed = carry
            slot = owner[parents[m, p]] if upper else owner[parents[parent, kid_pattern[m, p]]]
            slot_col, slot_row = slot // lay.col_slots, slot // lay.row_slots
            col_count[slot_col] = col_count[slot_col] + 1
            row_count[slot_row] = row_count[slot_row] + 1
            mine_col, mine_row = slot_col == col, slot_row == row
            source = m * (lay.length + upper_lead) + p + upper_lead

            @pl.when(mine_col)
            def _():
                at_block[blocks] = slot - col * lay.col_slots

                @pl.when(blocks < held)
                def _():
                    copy_to(send.at[blocks], source, blocks).start()

                if spill is not None:

                    @pl.when(blocks >= held)
                    def _():
                        copy_to(spill.at[blocks - held], source, blocks).start()

            @pl.when(mine_row)
            def _():
                local = slot - row * lay.row_slots
                base = lay.y_at + 4 * listed
                tab[base] = m
                tab[base + 1] = local
                tab[base + 2] = jnp.where(mine_col, blocks, -1)
                tab[base + 3] = parent
                tab[lay.out_at + m * lay.row_slots + local] = listed

            return blocks + mine_col.astype(jnp.int32), listed + mine_row.astype(jnp.int32)

        blocks, listed = lax.fori_loop(0, lay.length, visit, (blocks, listed))

        def each_row(y, count):
            local = tab[lay.y_at + 4 * y + 1]

            def each_block(w, count):
                tab[lay.a_at + count] = local * lay.col_slots + at_block[w]
                tab[lay.w_at + count] = w
                tab[lay.p_at + count] = y
                return count + 1

            return lax.fori_loop(first_block, blocks, each_block, count)

        products = lax.fori_loop(first_row, listed, each_row, products)
    tab[0] = products
    tab[1] = listed
    tab[2] = blocks
    tab[3] = 0
    most_col, most_row = col_count[0], row_count[0]
    for i in range(1, lay.cols):
        most_col = jnp.maximum(most_col, col_count[i])
    for i in range(1, lay.rows):
        most_row = jnp.maximum(most_row, row_count[i])
    most[0] = most_col + lay.lead
    most[1] = most_row

    def land(i, _):
        copy_to(send.at[0], 0, i).wait()
        return 0

    lax.fori_loop(0, blocks, land, 0)


def plan(lay, upper, here, owner, parents, kid_parent, kid_pattern, factor):
    block = factor.shape[2:]
    spilled = lay.full_w - lay.cap_w
    outs = [
        jax.ShapeDtypeStruct((lay.size,), jnp.int32),
        jax.ShapeDtypeStruct((2,), jnp.int32),
        jax.ShapeDtypeStruct((lay.cap_w,) + block, jnp.float32),
    ]
    specs = [SMEM, SMEM, HBM]
    if spilled:
        outs.append(jax.ShapeDtypeStruct((spilled,) + block, jnp.float32))
        specs.append(HBM)

    def body(*refs):
        refs = list(refs)
        if not spilled:
            refs.insert(9, None)
        plan_kernel(lay, upper, *refs)

    got = pl.pallas_call(
        body,
        out_shape=outs,
        in_specs=[SMEM] * 5 + [HBM],
        out_specs=specs,
        scratch_shapes=[
            pltpu.SMEM((lay.cols,), jnp.int32),
            pltpu.SMEM((lay.rows,), jnp.int32),
            pltpu.SMEM((lay.full_w,), jnp.int32),
            pltpu.SemaphoreType.DMA((lay.full_w,)),
        ],
        compiler_params=pltpu.CompilerParams(vmem_limit_bytes=VMEM_LIMIT),
    )(here, owner, parents, kid_parent, kid_pattern, factor)
    return got if spilled else list(got) + [None]


def halves(x):
    high = x.astype(jnp.bfloat16)
    return high, (x - high.astype(jnp.float32)).astype(jnp.bfloat16)


def dot3(a, b, dims):
    f = functools.partial(lax.dot_general, dimension_numbers=(dims, ((), ())), preferred_element_type=jnp.float32)
    return f(a[0], b[0]) + (f(a[0], b[1]) + f(a[1], b[0]))


PLAIN = ((1,), (0,))
TURNED = ((0,), (0,))


def mult_kernel(lay, pieces, here, tab, ancestors, *refs):
    bufs, (y, w, high, low, slots, w_sems, a_sems) = refs[: lay.rows * pieces], refs[lay.rows * pieces :]
    row = here[0]
    copies = []
    for piece in range(pieces):
        start = 0 if piece == 0 else lay.cap_w
        for k in range(lay.rows):
            buf = bufs[piece * lay.rows + k]
            depth = buf.shape[1]
            owner = lax.rem(row - k + lay.rows, lay.rows)
            target = w.at[pl.ds(start, buf.shape[0]), pl.ds(pl.multiple_of(owner * depth, depth), depth), :]
            copies.append(pltpu.make_async_copy(buf, target, w_sems.at[piece * lay.rows + k]))
    for copy in copies:
        copy.start()
    products, blocks = tab[0], tab[2]

    def fetch(i):
        block = tab[lay.a_at + i]
        source = ancestors.at[block // lay.col_slots, block % lay.col_slots]
        return pltpu.make_async_copy(source, slots.at[lax.rem(i, DEPTH)], a_sems.at[lax.rem(i, DEPTH)])

    def fetch_next(i):
        @pl.when(i < products)
        def _():
            fetch(i).start()

    for i in range(DEPTH - 1):
        fetch_next(jnp.int32(i))
    y[...] = jnp.zeros_like(y)
    for copy in copies:
        copy.wait()

    def split(i, _):
        high[i], low[i] = halves(w[i])
        return 0

    lax.fori_loop(lay.lead, blocks, split, 0)

    def step(i, _):
        fetch_next(i + DEPTH - 1)
        fetch(i).wait()
        at, to = tab[lay.w_at + i], tab[lay.p_at + i]
        y[to] += dot3(halves(slots[lax.rem(i, DEPTH)]), (high[at], low[at]), PLAIN)
        return 0

    lax.fori_loop(0, products, step, 0)


def mult(lay, cap_w, cap_y, here, tab, ancestors, bufs):
    size = ancestors.shape[2]
    pieces = len(bufs) // lay.rows
    return pl.pallas_call(
        functools.partial(mult_kernel, lay, pieces),
        out_shape=[
            jax.ShapeDtypeStruct((cap_y, size, size), jnp.float32),
            jax.ShapeDtypeStruct((cap_w, size, size), jnp.float32),
        ],
        in_specs=[SMEM, SMEM, HBM] + [HBM] * len(bufs),
        out_specs=[VMEM, VMEM],
        scratch_shapes=[
            pltpu.VMEM((cap_w, size, size), jnp.bfloat16),
            pltpu.VMEM((cap_w, size, size), jnp.bfloat16),
            pltpu.VMEM((DEPTH, size, size), jnp.float32),
            pltpu.SemaphoreType.DMA((len(bufs),)),
            pltpu.SemaphoreType.DMA((DEPTH,)),
        ],
        compiler_params=pltpu.CompilerParams(vmem_limit_bytes=VMEM_LIMIT),
        cost_estimate=pl.CostEstimate(flops=10**9, bytes_accessed=2 * 10**7, transcendentals=0),
    )(here, tab, ancestors, *bufs)


def spread_kernel(lay, extra, tab, own, other, w, *refs):
    add, (cov, term) = (refs[0], refs[1:]) if extra else (None, refs)
    term[...] = jnp.zeros_like(term)
    for m in range(lay.count):
        for s in range(lay.row_slots):
            place = tab[lay.out_at + m * lay.row_slots + s]

            @pl.when(place < 0)
            def _():
                cov[m, s] = jnp.zeros(cov.shape[2:], jnp.float32)

    def step(y, _):
        base = lay.y_at + 4 * y
        m, s, at = tab[base], tab[base + 1], tab[base + 2]
        total = own[y] + other[y]
        if extra:
            total = total + add[y]
        cov[m, s] = -total

        @pl.when(at >= 0)
        def _():
            term[m] += dot3(halves(w[at]), halves(total), TURNED)

        return 0

    lax.fori_loop(0, tab[1], step, 0)


def spread(lay, tab, own, other, w, add=None):
    size = own.shape[1]
    more = [] if add is None else [add]
    return pl.pallas_call(
        functools.partial(spread_kernel, lay, add is not None),
        out_shape=[
            jax.ShapeDtypeStruct((lay.count, lay.row_slots, size, size), jnp.float32),
            jax.ShapeDtypeStruct((lay.count, size, size), jnp.float32),
        ],
        in_specs=[SMEM] + [VMEM] * (3 + len(more)),
        out_specs=[VMEM, VMEM],
        compiler_params=pltpu.CompilerParams(vmem_limit_bytes=VMEM_LIMIT),
        cost_estimate=pl.CostEstimate(flops=10**9, bytes_accessed=10**7, transcendentals=0),
    )(tab, own, other, w, *more)


def cross_kernel(lay, tab, cov, w, through, upper):
    upper[...] = jnp.zeros_like(upper)

    def step(y, _):
        base = lay.y_at + 4 * y
        m, s, at, parent = tab[base], tab[base + 1], tab[base + 2], tab[base + 3]
        block = halves(cov[parent, s])
        through[y] = dot3(block, halves(w[m]), PLAIN)

        @pl.when(at >= 0)
        def _():
            upper[m] += dot3(block, halves(w[at]), TURNED)

        return 0

    lax.fori_loop(0, tab[1], step, 0)


def cross(lay, cap_y, tab, cov, w):
    size = w.shape[1]
    return pl.pallas_call(
        functools.partial(cross_kernel, lay),
        out_shape=[
            jax.ShapeDtypeStruct((cap_y, size, size), jnp.float32),
            jax.ShapeDtypeStruct((lay.count, size, size), jnp.float32),
        ],
        in_specs=[SMEM, VMEM, VMEM],
        out_specs=[VMEM, VMEM],
        compiler_params=pltpu.CompilerParams(vmem_limit_bytes=VMEM_LIMIT),
        cost_estimate=pl.CostEstimate(flops=10**9, bytes_accessed=10**7, transcendentals=0),
    )(tab, cov, w)


def shift(x, axis, size, by):
    return lax.ppermute(x, axis, [(i, (i + by) % size) for i in range(size)])


def ring(x, rows):
    out = [x]
    for _ in range(rows - 1):
        out.append(shift(out[-1], "row", rows, 1))
    return out


def other_half(x, cols):
    if cols == 2:
        return shift(x, "col", 2, 1)
    return lax.psum(x, "col") - x


def total(x, rows, cols):
    if cols != 2 or x.shape[0] != 2 or rows > 4:
        return lax.psum(x, ("row", "col"))
    row, col = lax.axis_index("row"), lax.axis_index("col")
    mine = lax.dynamic_index_in_dim(x, col, 0, False) + shift(lax.dynamic_index_in_dim(x, 1 - col, 0, False), "col", 2, 1)
    parts = mine.reshape(rows, -1, mine.shape[1])
    chunk = lax.dynamic_index_in_dim(parts, row, 0, False)
    arrived = [
        shift(lax.dynamic_index_in_dim(parts, lax.rem(row + d, rows), 0, False), "row", rows, d) for d in range(1, rows)
    ]
    for piece in arrived:
        chunk = chunk + piece
    pieces = [chunk] + [shift(chunk, "row", rows, d) for d in range(1, rows)]
    ordered = jnp.stack(pieces[::-1])
    mine = jnp.concatenate([ordered, ordered])
    mine = lax.dynamic_slice_in_dim(mine, rows - 1 - row, rows, 0).reshape(x.shape[1:])
    theirs = shift(mine, "col", 2, 1)
    return jnp.stack([jnp.where(col == 0, mine, theirs), jnp.where(col == 0, theirs, mine)])


def per_device(
    rows,
    cols,
    others,
    ancestor_cov,
    owner_slot,
    parent_pattern,
    parent_factor,
    parent_inverse,
    child_parent,
    child_pattern,
    child_factor,
    child_inverse,
):
    row_slots, col_slots = ancestor_cov.shape[:2]
    up = Layout(*parent_pattern.shape, 0, row_slots, col_slots, rows, cols)
    low = Layout(*child_pattern.shape, child_pattern.shape[0], row_slots, col_slots, rows, cols)
    here = jnp.stack([lax.axis_index("row"), lax.axis_index("col")]).astype(jnp.int32)
    index = (here, owner_slot, parent_pattern, child_parent, child_pattern)
    up_tab, up_most, up_send, up_spill = plan(up, True, *index, parent_factor)
    low_tab, low_most, low_send, low_spill = plan(low, False, *index, child_factor)
    up_bufs = ring(up_send, rows)
    most = jnp.concatenate([up_most, low_most])
    for axis, size in others:
        seen = most
        for by in range(1, size):
            most = jnp.maximum(most, shift(seen, axis, size, by))
    limits = (up.cap_w, up.cap_y, low.cap_w, low.cap_y)
    over = jnp.any(most > jnp.array(limits, jnp.int32))

    def rest(small, args):
        (here, ancestors, up_tab, low_tab, up_bufs, up_spill, low_send, low_spill, inverses, kid_parent) = args
        up_bufs = list(up_bufs)
        low_bufs = ring(low_send, rows)
        if not small:
            if up_spill is not None:
                up_bufs = up_bufs + ring(up_spill, rows)
            if low_spill is not None:
                low_bufs = low_bufs + ring(low_spill, rows)
        up_caps = (up.cap_w, up.cap_y) if small else (up.full_w, up.full_y)
        low_caps = (low.cap_w, low.cap_y) if small else (low.full_w, low.full_y)
        up_own, up_w = mult(up, *up_caps, here, up_tab, ancestors, up_bufs)
        up_other = other_half(up_own, cols)
        low_own, low_w = mult(low, *low_caps, here, low_tab, ancestors, low_bufs)
        low_other = other_half(low_own, cols)
        parent_cov, up_term = spread(up, up_tab, up_own, up_other, up_w)
        through, upper_part = cross(low, low_caps[1], low_tab, parent_cov, low_w)
        parent_diag = inverses[0] - total(up_term, rows, cols)
        upper_sum = total(upper_part, rows, cols)
        lead = low_w[: low.count]
        kid_diag = jnp.stack([lax.dynamic_index_in_dim(parent_diag, kid_parent[k], 0, False) for k in range(low.count)])
        upper = jnp.einsum("kxy,kyz->kxz", kid_diag, lead, precision=HIGH) + upper_sum
        diag = inverses[1] - jnp.einsum("kxy,kxz->kyz", lead, upper, precision=HIGH)
        child_cov, low_term = spread(low, low_tab, low_own, low_other, low_w, through)
        child_diag = diag - total(low_term, rows, cols)
        return parent_cov, parent_diag, child_cov, -upper, child_diag

    args = (
        here,
        ancestor_cov,
        up_tab,
        low_tab,
        tuple(up_bufs),
        up_spill,
        low_send,
        low_spill,
        (parent_inverse, child_inverse),
        child_parent,
    )
    return lax.cond(over, functools.partial(rest, False), functools.partial(rest, True), args)


def solution(mesh):
    in_specs = (
        P(("parts", "row"), "col", None, None),
        P("parts"),
        P(("parts", "sub"), None),
        P(("parts", "sub"), None, "row", None),
        P(("parts", "sub"), None, None),
        P(("parts", "sub")),
        P(("parts", "sub"), None),
        P(("parts", "sub"), None, "row", None),
        P(("parts", "sub"), None, None),
    )
    out_specs = (
        P(("parts", "sub"), "row", None, None),
        P(("parts", "sub"), None, None),
        P(("parts", "sub"), "row", None, None),
        P(("parts", "sub"), None, None),
        P(("parts", "sub"), None, None),
    )
    others = tuple((axis, mesh.shape[axis]) for axis in ("sub", "parts"))
    body = functools.partial(per_device, mesh.shape["row"], mesh.shape["col"], others)
    return jax.shard_map(body, mesh=mesh, in_specs=in_specs, out_specs=out_specs, check_vma=False)
```

```python
import functools

import jax
import jax.numpy as jnp
from jax import lax
from jax.experimental import pallas as pl
from jax.experimental.pallas import tpu as pltpu
from jax.sharding import PartitionSpec as P

VMEM_LIMIT = 50 * 1024 * 1024
FILL = 0
DEPTH = 16
SPARE = ((3, 3), (5, 5))
SMEM = pl.BlockSpec(memory_space=pltpu.SMEM)
VMEM = pl.BlockSpec(memory_space=pltpu.VMEM)
HBM = pl.BlockSpec(memory_space=pl.ANY)
PARAMS = pltpu.CompilerParams(vmem_limit_bytes=VMEM_LIMIT)


def cost(us):
    return pl.CostEstimate(flops=int(us * 1e7), bytes_accessed=int(us * 3.5e4), transcendentals=0)


class Layout:
    def __init__(self, count, length, lead, row_slots, col_slots, rows, cols):
        self.count, self.length, self.lead = count, length, lead
        self.row_slots, self.col_slots, self.rows, self.cols = row_slots, col_slots, rows, cols
        total = count * length
        self.whole = count * (length + lead)
        self.fill = 0 if cols != 2 else min(FILL, self.whole // 2) if lead else self.whole // 2
        self.full_y = count * min(length, row_slots)
        self.mean_y = -(-total // rows)
        products = self.full_y * min(total, count * min(length, col_slots))
        self.y_at = 4
        self.out_at = self.y_at + 4 * self.full_y
        self.a_at = self.out_at + count * row_slots
        self.w_at = self.a_at + products
        self.p_at = self.w_at + products
        self.used_at = self.p_at + products
        self.size = self.used_at + total

    def cap_y(self, spare):
        return min(self.full_y, self.mean_y + spare)


def plan_kernel(lay, above, here, owner, parents, kid_parent, kid_pattern, *refs):
    up_tab, refs = (None, refs) if above is None else (refs[0], refs[1:])
    tab, most, row_count, at_block = refs
    row, col = here[0], here[1]
    upper = above is None
    for i in range(lay.rows):
        row_count[i] = 0

    def clear(i, _):
        tab[lay.out_at + i] = -1
        return 0

    lax.fori_loop(0, lay.count * lay.row_slots, clear, 0)
    used, listed, products = jnp.int32(0), jnp.int32(0), jnp.int32(0)
    for m in range(lay.count):
        parent = m if upper else kid_parent[m]
        first_used, first_listed = used, listed

        def place(p, carry):
            used, listed = carry
            slot = owner[parents[parent, p if upper else kid_pattern[m, p]]]
            slot_col, slot_row = slot // lay.col_slots, slot // lay.row_slots
            row_count[slot_row] = row_count[slot_row] + 1
            mine_col, mine_row = slot_col == col, slot_row == row
            at = m * (lay.length + lay.lead) + lay.lead + p

            @pl.when(mine_col)
            def _():
                at_block[used] = slot - col * lay.col_slots
                tab[lay.used_at + used] = at

            @pl.when(mine_row)
            def _():
                local = slot - row * lay.row_slots
                base = lay.y_at + 4 * listed
                tab[base] = m
                tab[base + 1] = local
                tab[base + 2] = at
                tab[base + 3] = 0 if upper else up_tab[above.out_at + parent * lay.row_slots + local]
                tab[lay.out_at + m * lay.row_slots + local] = listed

            return used + mine_col.astype(jnp.int32), listed + mine_row.astype(jnp.int32)

        used, listed = lax.fori_loop(0, lay.length, place, (used, listed))

        def each_row(y, count):
            local = tab[lay.y_at + 4 * y + 1]

            def each_block(w, count):
                tab[lay.a_at + count] = local * lay.col_slots + at_block[w]
                tab[lay.w_at + count] = w
                tab[lay.p_at + count] = y
                return count + 1

            return lax.fori_loop(first_used, used, each_block, count)

        products = lax.fori_loop(first_listed, listed, each_row, products)
    most_row = row_count[0]
    for i in range(1, lay.rows):
        most_row = jnp.maximum(most_row, row_count[i])
    most[0] = most_row
    tab[0] = products
    tab[1] = listed
    tab[2] = used
    tab[3] = 0


def plan(lay, index, above=None, up_tab=None):
    return pl.pallas_call(
        functools.partial(plan_kernel, lay, above),
        out_shape=[jax.ShapeDtypeStruct((lay.size,), jnp.int32), jax.ShapeDtypeStruct((1,), jnp.int32)],
        in_specs=[SMEM] * (5 + (above is not None)),
        out_specs=[SMEM, SMEM],
        scratch_shapes=[pltpu.SMEM((lay.rows,), jnp.int32), pltpu.SMEM((lay.count * lay.length,), jnp.int32)],
        compiler_params=PARAMS,
        cost_estimate=cost(3),
    )(*index, *([] if above is None else [up_tab]))


PLAIN = ((1,), (0,))
TURNED = ((0,), (0,))


def left(x, axis):
    high = x.astype(jnp.bfloat16)
    low = (x - high.astype(jnp.float32)).astype(jnp.bfloat16)
    return jnp.concatenate([high, high, low], axis=axis)


def right(x):
    high = x.astype(jnp.bfloat16)
    low = (x - high.astype(jnp.float32)).astype(jnp.bfloat16)
    return jnp.concatenate([high, low, high], axis=0)


def dot(a, b, dims):
    return lax.dot_general(a, b, (dims, ((), ())), preferred_element_type=jnp.float32)


class Blocks:
    def __init__(self, lay, here, sizes, refs):
        self.row, self.rows = here[0], lay.rows
        if lay.fill:
            own, middle, other = sizes
            first = here[1] == 0
            at = lay.whole - lay.fill
            starts = [jnp.where(first, 0, at), lay.fill, jnp.where(first, at, 0)]
            groups = [own, middle, other]
        else:
            starts, groups = [0], [sizes[0]]
        self.places, self.arrays, i = [], [], 0
        for start, group in zip(starts, groups):
            for size in group:
                self.places.append((start, size))
                self.arrays.append(refs[i : i + lay.rows])
                start = start + size
                i += lay.rows

    def copies(self, at, target, sems, act):
        for (start, size), arrays in zip(self.places, self.arrays):

            @pl.when(jnp.logical_and(at >= start, at < start + size))
            def _():
                for k in range(self.rows):
                    depth = arrays[k].shape[1]
                    owner = lax.rem(self.row - k + self.rows, self.rows)
                    rows = pl.ds(pl.multiple_of(owner * depth, depth), depth)
                    act(pltpu.make_async_copy(arrays[k].at[at - start], target.at[rows, :], sems.at[k]))


def flatten(pieces):
    sizes = tuple(tuple(part[0].shape[0] for part in group) for group in pieces)
    return sizes, [x for group in pieces for part in group for x in part]


def mult_kernel(lay, sizes, here, tab, ancestors, *refs):
    above, refs = (refs[0], refs[1:]) if lay.lead else (None, refs)
    blocks = Blocks(lay, here, sizes, refs[:-6])
    y, w, wide, slots, w_sems, a_sems = refs[-6:]
    products, used, listed = tab[0], tab[2], tab[1]
    leads = lay.count * lay.length

    def load(i, act):
        blocks.copies(tab[lay.used_at + i], w.at[i], w_sems.at[i], act)

    def start(copy):
        copy.start()

    def wait(copy):
        copy.wait()

    for m in range(lay.count * lay.lead):
        blocks.copies(jnp.int32(m * (lay.length + lay.lead)), w.at[leads + m], w_sems.at[leads + m], start)

    def begin(i, _):
        load(i, start)
        return 0

    lax.fori_loop(0, used, begin, 0)

    def fetch(i):
        block = tab[lay.a_at + i]
        source = ancestors.at[block // lay.col_slots, block % lay.col_slots]
        return pltpu.make_async_copy(source, slots.at[lax.rem(i, DEPTH)], a_sems.at[lax.rem(i, DEPTH)])

    def fetch_next(i):
        @pl.when(i < products)
        def _():
            fetch(i).start()

    for i in range(DEPTH - 1):
        fetch_next(jnp.int32(i))
    y[...] = jnp.zeros_like(y)

    if lay.lead:
        for m in range(lay.count):
            blocks.copies(jnp.int32(m * (lay.length + lay.lead)), w.at[leads + m], w_sems.at[leads + m], wait)

        def through(i, _):
            base = lay.y_at + 4 * i
            m, up = tab[base], tab[base + 3]
            y[i] = -dot(left(above[up], 1), right(w[leads + m]), PLAIN)
            return 0

        lax.fori_loop(0, listed, through, 0)

    def spread_out(i, _):
        load(i, wait)
        wide[i] = right(w[i])
        return 0

    lax.fori_loop(0, used, spread_out, 0)

    def step(i, _):
        fetch_next(i + DEPTH - 1)
        fetch(i).wait()
        y[tab[lay.p_at + i]] += dot(left(slots[lax.rem(i, DEPTH)], 1), wide[tab[lay.w_at + i]], PLAIN)
        return 0

    lax.fori_loop(0, products, step, 0)


def mult(lay, cap_y, here, tab, ancestors, pieces, above=None):
    size = ancestors.shape[2]
    sizes, bufs = flatten(pieces)
    held = lay.count * (lay.length + lay.lead)
    return pl.pallas_call(
        functools.partial(mult_kernel, lay, sizes),
        out_shape=jax.ShapeDtypeStruct((cap_y, size, size), jnp.float32),
        in_specs=[SMEM, SMEM, HBM] + [VMEM] * lay.lead + [HBM] * len(bufs),
        out_specs=VMEM,
        scratch_shapes=[
            pltpu.VMEM((held, size, size), jnp.float32),
            pltpu.VMEM((lay.count * lay.length, 3 * size, size), jnp.bfloat16),
            pltpu.VMEM((DEPTH, size, size), jnp.float32),
            pltpu.SemaphoreType.DMA((held, lay.rows)),
            pltpu.SemaphoreType.DMA((DEPTH,)),
        ],
        compiler_params=PARAMS,
        cost_estimate=cost(20),
    )(here, tab, ancestors, *([] if above is None else [above]), *bufs)


def put_chunks(row, rows, total, outs):
    depth = outs[0].shape[1]
    for d in range(rows):
        at = lax.rem(row + d, rows)
        outs[d][...] = total[:, pl.ds(pl.multiple_of(at * depth, depth), depth), :]


def chunk_shapes(count, rows, size):
    return [jax.ShapeDtypeStruct((count, size // rows, size), jnp.float32)] * rows


def spread_kernel(lay, tab, own, *refs):
    parts, cov = refs[:-1], refs[-1]
    for m in range(lay.count):
        for s in range(lay.row_slots):
            place = tab[lay.out_at + m * lay.row_slots + s]

            @pl.when(place < 0)
            def _():
                cov[m, s] = jnp.zeros(cov.shape[2:], jnp.float32)

            at = 0
            for part in parts:
                here = jnp.logical_and(place >= at, place < at + part.shape[0])

                @pl.when(here)
                def _():
                    cov[m, s] = -(own[place] + part[place - at])

                at += part.shape[0]


def spread(lay, tab, own, parts):
    size = own.shape[1]
    return pl.pallas_call(
        functools.partial(spread_kernel, lay),
        out_shape=jax.ShapeDtypeStruct((lay.count, lay.row_slots, size, size), jnp.float32),
        in_specs=[SMEM] + [VMEM] * (1 + len(parts)),
        out_specs=VMEM,
        compiler_params=PARAMS,
        cost_estimate=cost(1),
    )(tab, own, *parts)


def terms_kernel(lay, sizes, here, tab, own, *refs):
    above, refs = (refs[0], refs[1:]) if lay.lead else (None, refs)
    w, term, sems = refs[-3:]
    lead, refs = (refs[-4], refs[:-4]) if lay.lead else (None, refs[:-3])
    outs = refs[-lay.rows :]
    blocks = Blocks(lay, here, sizes, refs[: -lay.rows])
    listed = tab[1]

    def load(i, act):
        blocks.copies(tab[lay.y_at + 4 * i + 2], w.at[i], sems.at[i], act)

    def start(copy):
        copy.start()

    def wait(copy):
        copy.wait()

    def begin(i, _):
        load(i, start)
        return 0

    lax.fori_loop(0, listed, begin, 0)
    for m in range(lay.count * lay.lead):
        blocks.copies(jnp.int32(m * (lay.length + lay.lead)), lead.at[m], sems.at[lay.full_y + m], start)
    term[...] = jnp.zeros_like(term)

    def step(y, _):
        load(y, wait)
        base = lay.y_at + 4 * y
        m = tab[base]
        block = w[y]
        term[m] += dot(left(block, 0), right(own[y]), TURNED)
        if lay.lead:
            term[lay.count + m] -= dot(left(above[tab[base + 3]], 0), right(block), TURNED)
        return 0

    lax.fori_loop(0, listed, step, 0)
    for m in range(lay.count * lay.lead):
        blocks.copies(jnp.int32(m * (lay.length + lay.lead)), lead.at[m], sems.at[lay.full_y + m], wait)
    put_chunks(here[0], lay.rows, term, outs)


def terms(lay, here, tab, own, pieces, above=None):
    size = own.shape[1]
    sizes, bufs = flatten(pieces)
    sums = lay.count * (1 + lay.lead)
    outs = chunk_shapes(sums, lay.rows, size) + [jax.ShapeDtypeStruct((lay.count, size, size), jnp.float32)] * lay.lead
    got = pl.pallas_call(
        functools.partial(terms_kernel, lay, sizes),
        out_shape=outs,
        in_specs=[SMEM, SMEM] + [VMEM] * (1 + lay.lead) + [HBM] * len(bufs),
        out_specs=[VMEM] * len(outs),
        scratch_shapes=[
            pltpu.VMEM((lay.full_y, size, size), jnp.float32),
            pltpu.VMEM((sums, size, size), jnp.float32),
            pltpu.SemaphoreType.DMA((lay.full_y + lay.count, lay.rows)),
        ],
        compiler_params=PARAMS,
        cost_estimate=cost(1),
    )(here, tab, own, *([] if above is None else [above]), *bufs)
    return list(got[: lay.rows]), got[-1]


def finish_kernel(rows, count, here, kid_parent, *refs):
    up_pieces, low_pieces = refs[:rows], refs[rows : 2 * rows]
    inverse, kid_inverse, lead, diag, upper, kid_diag, sums, sems = refs[2 * rows :]
    depth = up_pieces[0].shape[1]
    copies = []
    for k in range(rows):
        at = pl.ds(pl.multiple_of(lax.rem(here[0] - k + rows, rows) * depth, depth), depth)
        copies.append(pltpu.make_async_copy(up_pieces[k], diag.at[:, at, :], sems.at[k]))
        copies.append(pltpu.make_async_copy(low_pieces[k], sums.at[:, at, :], sems.at[rows + k]))
    for copy in copies:
        copy.start()
    for copy in copies:
        copy.wait()
    diag[...] = inverse[...] - diag[...]
    for k in range(count):
        v = right(lead[k])
        z = dot(left(diag[kid_parent[k]], 1), v, PLAIN) + sums[count + k]
        upper[k] = -z
        kid_diag[k] = kid_inverse[k] - dot(left(lead[k], 0), right(z), TURNED) - sums[k]


def finish(rows, here, kid_parent, up_pieces, low_pieces, inverse, kid_inverse, lead):
    return pl.pallas_call(
        functools.partial(finish_kernel, rows, lead.shape[0]),
        out_shape=[
            jax.ShapeDtypeStruct(inverse.shape, jnp.float32),
            jax.ShapeDtypeStruct(kid_inverse.shape, jnp.float32),
            jax.ShapeDtypeStruct(kid_inverse.shape, jnp.float32),
        ],
        in_specs=[SMEM, SMEM] + [HBM] * (2 * rows) + [VMEM] * 3,
        out_specs=[VMEM] * 3,
        scratch_shapes=[
            pltpu.VMEM((low_pieces[0].shape[0],) + lead.shape[1:], jnp.float32),
            pltpu.SemaphoreType.DMA((2 * rows,)),
        ],
        compiler_params=PARAMS,
        cost_estimate=cost(1),
    )(here, kid_parent, *up_pieces, *low_pieces, inverse, kid_inverse, lead)


def shift(x, axis, size, by):
    return lax.ppermute(x, axis, [(i, (i + by) % size) for i in range(size)])


def after(x, *others):
    return lax.optimization_barrier((x,) + others)[0]


def ring(x, rows):
    out = [x]
    for _ in range(rows - 1):
        out.append(shift(out[-1], "row", rows, 1))
    return out


def filled_ring(x, fill, rows):
    first = lax.axis_index("col") == 0
    low, high = x[:fill], x[-fill:]
    mine, theirs = [jnp.where(first, low, high)], [jnp.where(first, high, low)]
    middle = [x[fill:-fill]]
    for step in range(rows - 1):
        send = after(mine[-1], *(theirs[step - 1 : step] if step > 1 else ()))
        mine.append(shift(send, "row", rows, 1))
        if middle[0].shape[0]:
            middle.append(shift(middle[-1], "row", rows, 1))
        if step:
            theirs.append(shift(mine[step], "col", 2, 1))
    theirs.append(shift(mine[-1], "col", 2, 1))
    return [[mine], [middle] if middle[0].shape[0] else [], [theirs]]


def swapped(x, cols):
    if cols == 2:
        return shift(x, "col", 2, 1)
    return lax.psum(x, "col") - x


def scatter_sums(chunks, rows):
    mine = chunks[0]
    for piece in [shift(chunks[d], "row", rows, d) for d in range(1, rows)]:
        mine = mine + piece
    return mine


def collect(mine, rows):
    return [mine] + [shift(mine, "row", rows, d) for d in range(1, rows)]


def per_device(
    rows,
    cols,
    others,
    ancestor_cov,
    owner_slot,
    parent_pattern,
    parent_factor,
    parent_inverse,
    child_parent,
    child_pattern,
    child_factor,
    child_inverse,
):
    row_slots, col_slots = ancestor_cov.shape[:2]
    up = Layout(*parent_pattern.shape, 0, row_slots, col_slots, rows, cols)
    low = Layout(*child_pattern.shape, 1, row_slots, col_slots, rows, cols)
    flat = lambda x: x.reshape((-1,) + x.shape[2:])
    up_pieces = filled_ring(flat(parent_factor), up.fill, rows) if up.fill else [[ring(flat(parent_factor), rows)]]
    here = jnp.stack([lax.axis_index("row"), lax.axis_index("col")]).astype(jnp.int32)
    index = (here, owner_slot, parent_pattern, child_parent, child_pattern)
    up_tab, up_most = plan(up, index)
    low_tab, low_most = plan(low, index, up, up_tab)
    most = jnp.concatenate([up_most, low_most])
    for axis, size in others:
        seen = most
        for by in range(1, size):
            most = jnp.maximum(most, shift(seen, axis, size, by))
    branch = jnp.int32(0)
    for up_spare, low_spare in SPARE:
        limits = jnp.array((up.cap_y(up_spare), low.cap_y(low_spare)), jnp.int32)
        branch = branch + jnp.any(most > limits).astype(jnp.int32)
    gate = [x[-1] for group in up_pieces[:1] for x in group] + [x[-2] for group in up_pieces[2:] for x in group]
    early = [flat(child_factor)]
    early.append(shift(after(early[0], *gate), "row", rows, 1))
    up_own = mult(up, up.full_y, here, up_tab, ancestor_cov, up_pieces)

    def rest(spare, args):
        here, ancestors, up_tab, low_tab, up_own, up_pieces, early, inverse, kid_inverse, kid_parent = args
        up_y, low_y = (up.full_y, low.full_y) if spare is None else (up.cap_y(spare[0]), low.cap_y(spare[1]))
        up_half, low_half = up_y // 2, low_y // 2
        kids = list(early)
        for _ in range(rows - 3):
            kids.append(shift(kids[-1], "row", rows, 1))
        up_other = [swapped(up_own[:up_half], cols)]
        up_parts, _ = terms(up, here, up_tab, up_own, up_pieces)
        kids.append(shift(after(kids[-1], up_other[0], *up_parts), "row", rows, 1))
        up_other.append(swapped(up_own[up_half:up_y], cols))
        low_own = mult(low, low_y, here, low_tab, after(ancestors, up_other[1]), [[kids]], up_own)
        up_sum = scatter_sums([after(x, kids[-1]) for x in up_parts], rows)
        theirs = swapped(after(up_sum, low_own), cols)
        low_other = [swapped(after(low_own[:low_half], theirs), cols)]
        low_parts, lead = terms(low, here, low_tab, low_own, [[kids]], up_own)
        up_pieces = collect(up_sum + theirs, rows)
        low_sum = scatter_sums(low_parts, rows)
        theirs = swapped(after(low_sum, low_other[0]), cols)
        low_other.append(swapped(after(low_own[low_half:], theirs), cols))
        low_pieces = collect(low_sum + theirs, rows)
        parent_cov = spread(up, up_tab, up_own, up_other)
        diag, upper, kid_diag = finish(rows, here, kid_parent, up_pieces, low_pieces, inverse, kid_inverse, lead)
        child_cov = spread(low, low_tab, low_own, low_other)
        return parent_cov, diag, child_cov, upper, kid_diag

    args = (
        here,
        ancestor_cov,
        up_tab,
        low_tab,
        up_own,
        up_pieces,
        early,
        parent_inverse,
        child_inverse,
        child_parent,
    )
    return lax.switch(branch, [functools.partial(rest, spare) for spare in SPARE + (None,)], args)


def solution(mesh):
    in_specs = (
        P(("parts", "row"), "col", None, None),
        P("parts"),
        P(("parts", "sub"), None),
        P(("parts", "sub"), None, "row", None),
        P(("parts", "sub"), None, None),
        P(("parts", "sub")),
        P(("parts", "sub"), None),
        P(("parts", "sub"), None, "row", None),
        P(("parts", "sub"), None, None),
    )
    out_specs = (
        P(("parts", "sub"), "row", None, None),
        P(("parts", "sub"), None, None),
        P(("parts", "sub"), "row", None, None),
        P(("parts", "sub"), None, None),
        P(("parts", "sub"), None, None),
    )
    others = tuple((axis, mesh.shape[axis]) for axis in ("sub", "parts"))
    body = functools.partial(per_device, mesh.shape["row"], mesh.shape["col"], others)
    return jax.shard_map(body, mesh=mesh, in_specs=in_specs, out_specs=out_specs, check_vma=False)
```

```python
import functools

import jax
import jax.numpy as jnp
from jax import lax
from jax.experimental import pallas as pl
from jax.experimental.pallas import tpu as pltpu
from jax.sharding import PartitionSpec as P

VMEM_LIMIT = 50 * 1024 * 1024
FILL = 0
DEPTH = 16
SPARE = ((3, 4), (5, 6))
SMEM = pl.BlockSpec(memory_space=pltpu.SMEM)
VMEM = pl.BlockSpec(memory_space=pltpu.VMEM)
HBM = pl.BlockSpec(memory_space=pl.ANY)
PARAMS = pltpu.CompilerParams(vmem_limit_bytes=VMEM_LIMIT)


def cost(us):
    return pl.CostEstimate(flops=int(us * 1e7), bytes_accessed=int(us * 3.5e4), transcendentals=0)


class Layout:
    def __init__(self, count, length, lead, row_slots, col_slots, rows, cols):
        self.count, self.length, self.lead = count, length, lead
        self.row_slots, self.col_slots, self.rows, self.cols = row_slots, col_slots, rows, cols
        total = count * length
        self.whole = count * (length + lead)
        self.fill = 0 if cols != 2 else min(FILL, self.whole // 2) if lead else self.whole // 2
        self.full_y = count * min(length, row_slots)
        self.mean_y = -(-total // rows)
        products = self.full_y * (min(length, col_slots) + 1)
        self.y_at = 4
        self.out_at = self.y_at + 4 * self.full_y
        self.a_at = self.out_at + count * row_slots
        self.w_at = self.a_at + products
        self.p_at = self.w_at + products
        self.used_at = self.p_at + products
        self.size = self.used_at + total

    def cap_y(self, spare):
        return min(self.full_y, self.mean_y + spare)


def plan_kernel(lay, above, here, owner, parents, kid_parent, kid_pattern, *refs):
    up_tab, refs = (None, refs) if above is None else (refs[0], refs[1:])
    tab, most, row_count, at_block = refs
    row, col = here[0], here[1]
    upper = above is None
    for i in range(lay.rows):
        row_count[i] = 0

    def clear(i, _):
        tab[lay.out_at + i] = -1
        return 0

    lax.fori_loop(0, lay.count * lay.row_slots, clear, 0)
    used, listed, products = jnp.int32(0), jnp.int32(0), jnp.int32(0)
    for m in range(lay.count):
        parent = m if upper else kid_parent[m]
        first_used, first_listed = used, listed

        def place(p, carry):
            used, listed = carry
            slot = owner[parents[parent, p if upper else kid_pattern[m, p]]]
            slot_col, slot_row = slot // lay.col_slots, slot // lay.row_slots
            row_count[slot_row] = row_count[slot_row] + 1
            mine_col, mine_row = slot_col == col, slot_row == row
            at = m * (lay.length + lay.lead) + lay.lead + p

            @pl.when(mine_col)
            def _():
                at_block[used] = slot - col * lay.col_slots
                tab[lay.used_at + used] = at

            @pl.when(mine_row)
            def _():
                local = slot - row * lay.row_slots
                base = lay.y_at + 4 * listed
                tab[base] = m
                tab[base + 1] = local
                tab[base + 2] = at
                tab[base + 3] = 0 if upper else up_tab[above.out_at + parent * lay.row_slots + local]
                tab[lay.out_at + m * lay.row_slots + local] = listed

            return used + mine_col.astype(jnp.int32), listed + mine_row.astype(jnp.int32)

        used, listed = lax.fori_loop(0, lay.length, place, (used, listed))

        def each_row(y, count):
            local = tab[lay.y_at + 4 * y + 1]

            def each_block(w, count):
                tab[lay.a_at + count] = local * lay.col_slots + at_block[w]
                tab[lay.w_at + count] = w
                tab[lay.p_at + count] = y
                return count + 1

            count = lax.fori_loop(first_used, used, each_block, count)
            odd = lax.rem(used - first_used, 2)

            @pl.when(odd == 1)
            def _():
                tab[lay.a_at + count] = local * lay.col_slots
                tab[lay.w_at + count] = lay.count * lay.length
                tab[lay.p_at + count] = y

            return count + odd

        products = lax.fori_loop(first_listed, listed, each_row, products)
    most_row = row_count[0]
    for i in range(1, lay.rows):
        most_row = jnp.maximum(most_row, row_count[i])
    most[0] = most_row
    tab[0] = products
    tab[1] = listed
    tab[2] = used
    tab[3] = 0


def plan(lay, index, above=None, up_tab=None):
    return pl.pallas_call(
        functools.partial(plan_kernel, lay, above),
        out_shape=[jax.ShapeDtypeStruct((lay.size,), jnp.int32), jax.ShapeDtypeStruct((1,), jnp.int32)],
        in_specs=[SMEM] * (5 + (above is not None)),
        out_specs=[SMEM, SMEM],
        scratch_shapes=[pltpu.SMEM((lay.rows,), jnp.int32), pltpu.SMEM((lay.count * lay.length,), jnp.int32)],
        compiler_params=PARAMS,
        cost_estimate=cost(3),
    )(*index, *([] if above is None else [up_tab]))


PLAIN = ((1,), (0,))
TURNED = ((0,), (0,))


def left(x, axis):
    high = x.astype(jnp.bfloat16)
    low = (x - high.astype(jnp.float32)).astype(jnp.bfloat16)
    return jnp.concatenate([high, high, low], axis=axis)


def right(x):
    high = x.astype(jnp.bfloat16)
    low = (x - high.astype(jnp.float32)).astype(jnp.bfloat16)
    return jnp.concatenate([high, low, high], axis=0)


def dot(a, b, dims):
    return lax.dot_general(a, b, (dims, ((), ())), preferred_element_type=jnp.float32)


class Blocks:
    def __init__(self, lay, here, sizes, refs):
        self.row, self.rows = here[0], lay.rows
        if lay.fill:
            own, middle, other = sizes
            first = here[1] == 0
            at = lay.whole - lay.fill
            starts = [jnp.where(first, 0, at), lay.fill, jnp.where(first, at, 0)]
            groups = [own, middle, other]
        else:
            starts, groups = [0], [sizes[0]]
        self.places, self.arrays, i = [], [], 0
        for start, group in zip(starts, groups):
            for size in group:
                self.places.append((start, size))
                self.arrays.append(refs[i : i + lay.rows])
                start = start + size
                i += lay.rows

    def copies(self, at, target, sems, act):
        for (start, size), arrays in zip(self.places, self.arrays):

            @pl.when(jnp.logical_and(at >= start, at < start + size))
            def _():
                for k in range(self.rows):
                    depth = arrays[k].shape[1]
                    owner = lax.rem(self.row - k + self.rows, self.rows)
                    rows = pl.ds(pl.multiple_of(owner * depth, depth), depth)
                    act(pltpu.make_async_copy(arrays[k].at[at - start], target.at[rows, :], sems.at[k]))


def flatten(pieces):
    sizes = tuple(tuple(part[0].shape[0] for part in group) for group in pieces)
    return sizes, [x for group in pieces for part in group for x in part]


def mult_kernel(lay, sizes, parts, here, tab, ancestors, *refs):
    above, refs = (refs[0], refs[1:]) if lay.lead else (None, refs)
    blocks = Blocks(lay, here, sizes, refs[: -6 - parts])
    y, w, wide, slots, w_sems, a_sems = refs[-6 - parts : -5 - parts] + refs[-5:]
    pieces = refs[-5 - parts : -5]
    products, used, listed = tab[0], tab[2], tab[1]
    leads = lay.count * lay.length

    def load(i, act):
        blocks.copies(tab[lay.used_at + i], w.at[i], w_sems.at[i], act)

    def start(copy):
        copy.start()

    def wait(copy):
        copy.wait()

    for m in range(lay.count * lay.lead):
        blocks.copies(jnp.int32(m * (lay.length + lay.lead)), w.at[leads + m], w_sems.at[leads + m], start)

    def begin(i, _):
        load(i, start)
        return 0

    lax.fori_loop(0, used, begin, 0)

    def fetch(i):
        block = tab[lay.a_at + i]
        source = ancestors.at[block // lay.col_slots, block % lay.col_slots]
        return pltpu.make_async_copy(source, slots.at[lax.rem(i, DEPTH)], a_sems.at[lax.rem(i, DEPTH)])

    def fetch_next(i):
        @pl.when(i < products)
        def _():
            fetch(i).start()

    for i in range(DEPTH - 2):
        fetch_next(jnp.int32(i))
    y[...] = jnp.zeros_like(y)
    wide[lay.count * lay.length] = jnp.zeros(wide.shape[1:], jnp.bfloat16)

    if lay.lead:
        for m in range(lay.count):
            blocks.copies(jnp.int32(m * (lay.length + lay.lead)), w.at[leads + m], w_sems.at[leads + m], wait)

        def through(i, _):
            base = lay.y_at + 4 * i
            m, up = tab[base], tab[base + 3]
            y[i] = -dot(left(above[up], 1), right(w[leads + m]), PLAIN)
            return 0

        lax.fori_loop(0, listed, through, 0)

    def spread_out(i, _):
        load(i, wait)
        wide[i] = right(w[i])
        return 0

    lax.fori_loop(0, used, spread_out, 0)

    def step(i, _):
        one, two = 2 * i, 2 * i + 1
        fetch_next(one + DEPTH - 2)
        fetch_next(two + DEPTH - 2)
        fetch(one).wait()
        fetch(two).wait()
        first = dot(left(slots[lax.rem(one, DEPTH)], 1), wide[tab[lay.w_at + one]], PLAIN)
        second = dot(left(slots[lax.rem(two, DEPTH)], 1), wide[tab[lay.w_at + two]], PLAIN)
        y[tab[lay.p_at + one]] += first + second
        return 0

    lax.fori_loop(0, products // 2, step, 0)
    at = 0
    for piece in pieces:
        piece[...] = y[at : at + piece.shape[0]]
        at += piece.shape[0]


def mult(lay, cap_y, here, tab, ancestors, pieces, above=None, parts=()):
    size = ancestors.shape[2]
    sizes, bufs = flatten(pieces)
    held = lay.count * (lay.length + lay.lead)
    return pl.pallas_call(
        functools.partial(mult_kernel, lay, sizes, len(parts)),
        out_shape=[jax.ShapeDtypeStruct((n, size, size), jnp.float32) for n in (cap_y,) + tuple(parts)],
        in_specs=[SMEM, SMEM, HBM] + [VMEM] * lay.lead + [HBM] * len(bufs),
        out_specs=[VMEM] * (1 + len(parts)),
        scratch_shapes=[
            pltpu.VMEM((held, size, size), jnp.float32),
            pltpu.VMEM((lay.count * lay.length + 1, 3 * size, size), jnp.bfloat16),
            pltpu.VMEM((DEPTH, size, size), jnp.float32),
            pltpu.SemaphoreType.DMA((held, lay.rows)),
            pltpu.SemaphoreType.DMA((DEPTH,)),
        ],
        compiler_params=PARAMS,
        cost_estimate=cost(20),
    )(here, tab, ancestors, *([] if above is None else [above]), *bufs)


def put_chunks(row, rows, total, outs):
    depth = outs[0].shape[1]
    for d in range(rows):
        at = lax.rem(row + d, rows)
        outs[d][...] = total[:, pl.ds(pl.multiple_of(at * depth, depth), depth), :]


def chunk_shapes(count, rows, size):
    return [jax.ShapeDtypeStruct((count, size // rows, size), jnp.float32)] * rows


def spread_kernel(lay, tab, own, *refs):
    parts, cov = refs[:-1], refs[-1]
    for m in range(lay.count):
        for s in range(lay.row_slots):
            place = tab[lay.out_at + m * lay.row_slots + s]

            @pl.when(place < 0)
            def _():
                cov[m, s] = jnp.zeros(cov.shape[2:], jnp.float32)

            at = 0
            for part in parts:
                here = jnp.logical_and(place >= at, place < at + part.shape[0])

                @pl.when(here)
                def _():
                    cov[m, s] = -(own[place] + part[place - at])

                at += part.shape[0]


def spread(lay, tab, own, parts):
    size = own.shape[1]
    return pl.pallas_call(
        functools.partial(spread_kernel, lay),
        out_shape=jax.ShapeDtypeStruct((lay.count, lay.row_slots, size, size), jnp.float32),
        in_specs=[SMEM] + [VMEM] * (1 + len(parts)),
        out_specs=VMEM,
        compiler_params=PARAMS,
        cost_estimate=cost(1),
    )(tab, own, *parts)


def terms_kernel(lay, sizes, here, tab, own, *refs):
    above, refs = (refs[0], refs[1:]) if lay.lead else (None, refs)
    w, term, sems = refs[-3:]
    lead, refs = (refs[-4], refs[:-4]) if lay.lead else (None, refs[:-3])
    outs = refs[-lay.rows :]
    blocks = Blocks(lay, here, sizes, refs[: -lay.rows])
    listed = tab[1]

    def load(i, act):
        blocks.copies(tab[lay.y_at + 4 * i + 2], w.at[i], sems.at[i], act)

    def start(copy):
        copy.start()

    def wait(copy):
        copy.wait()

    def begin(i, _):
        load(i, start)
        return 0

    lax.fori_loop(0, listed, begin, 0)
    for m in range(lay.count * lay.lead):
        blocks.copies(jnp.int32(m * (lay.length + lay.lead)), lead.at[m], sems.at[lay.full_y + m], start)
    term[...] = jnp.zeros_like(term)

    def step(y, _):
        load(y, wait)
        base = lay.y_at + 4 * y
        m = tab[base]
        block = w[y]
        term[m] += dot(left(block, 0), right(own[y]), TURNED)
        if lay.lead:
            term[lay.count + m] -= dot(left(above[tab[base + 3]], 0), right(block), TURNED)
        return 0

    lax.fori_loop(0, listed, step, 0)
    for m in range(lay.count * lay.lead):
        blocks.copies(jnp.int32(m * (lay.length + lay.lead)), lead.at[m], sems.at[lay.full_y + m], wait)
    put_chunks(here[0], lay.rows, term, outs)


def terms(lay, here, tab, own, pieces, above=None):
    size = own.shape[1]
    sizes, bufs = flatten(pieces)
    sums = lay.count * (1 + lay.lead)
    outs = chunk_shapes(sums, lay.rows, size) + [jax.ShapeDtypeStruct((lay.count, size, size), jnp.float32)] * lay.lead
    got = pl.pallas_call(
        functools.partial(terms_kernel, lay, sizes),
        out_shape=outs,
        in_specs=[SMEM, SMEM] + [VMEM] * (1 + lay.lead) + [HBM] * len(bufs),
        out_specs=[VMEM] * len(outs),
        scratch_shapes=[
            pltpu.VMEM((lay.full_y, size, size), jnp.float32),
            pltpu.VMEM((sums, size, size), jnp.float32),
            pltpu.SemaphoreType.DMA((lay.full_y + lay.count, lay.rows)),
        ],
        compiler_params=PARAMS,
        cost_estimate=cost(1),
    )(here, tab, own, *([] if above is None else [above]), *bufs)
    return list(got[: lay.rows]), got[-1]


def finish_kernel(rows, count, here, kid_parent, *refs):
    up_pieces, low_pieces = refs[:rows], refs[rows : 2 * rows]
    inverse, kid_inverse, lead, diag, upper, kid_diag, sums, sems = refs[2 * rows :]
    depth = up_pieces[0].shape[1]
    copies = []
    for k in range(rows):
        at = pl.ds(pl.multiple_of(lax.rem(here[0] - k + rows, rows) * depth, depth), depth)
        copies.append(pltpu.make_async_copy(up_pieces[k], diag.at[:, at, :], sems.at[k]))
        copies.append(pltpu.make_async_copy(low_pieces[k], sums.at[:, at, :], sems.at[rows + k]))
    for copy in copies:
        copy.start()
    for copy in copies:
        copy.wait()
    diag[...] = inverse[...] - diag[...]
    for k in range(count):
        v = right(lead[k])
        z = dot(left(diag[kid_parent[k]], 1), v, PLAIN) + sums[count + k]
        upper[k] = -z
        kid_diag[k] = kid_inverse[k] - dot(left(lead[k], 0), right(z), TURNED) - sums[k]


def finish(rows, here, kid_parent, up_pieces, low_pieces, inverse, kid_inverse, lead):
    return pl.pallas_call(
        functools.partial(finish_kernel, rows, lead.shape[0]),
        out_shape=[
            jax.ShapeDtypeStruct(inverse.shape, jnp.float32),
            jax.ShapeDtypeStruct(kid_inverse.shape, jnp.float32),
            jax.ShapeDtypeStruct(kid_inverse.shape, jnp.float32),
        ],
        in_specs=[SMEM, SMEM] + [HBM] * (2 * rows) + [VMEM] * 3,
        out_specs=[VMEM] * 3,
        scratch_shapes=[
            pltpu.VMEM((low_pieces[0].shape[0],) + lead.shape[1:], jnp.float32),
            pltpu.SemaphoreType.DMA((2 * rows,)),
        ],
        compiler_params=PARAMS,
        cost_estimate=cost(1),
    )(here, kid_parent, *up_pieces, *low_pieces, inverse, kid_inverse, lead)


def shift(x, axis, size, by):
    return lax.ppermute(x, axis, [(i, (i + by) % size) for i in range(size)])


def after(x, *others):
    return lax.optimization_barrier((x,) + others)[0]


def ring(x, rows):
    out = [x]
    for _ in range(rows - 1):
        out.append(shift(out[-1], "row", rows, 1))
    return out


def filled_ring(x, fill, rows):
    first = lax.axis_index("col") == 0
    low, high = x[:fill], x[-fill:]
    mine, theirs = [jnp.where(first, low, high)], [jnp.where(first, high, low)]
    middle = [x[fill:-fill]]
    for step in range(rows - 1):
        send = after(mine[-1], *(theirs[step - 1 : step] if step > 1 else ()))
        mine.append(shift(send, "row", rows, 1))
        if middle[0].shape[0]:
            middle.append(shift(middle[-1], "row", rows, 1))
        if step:
            theirs.append(shift(mine[step], "col", 2, 1))
    theirs.append(shift(mine[-1], "col", 2, 1))
    return [[mine], [middle] if middle[0].shape[0] else [], [theirs]]


def swapped(x, cols):
    if cols == 2:
        return shift(x, "col", 2, 1)
    return lax.psum(x, "col") - x


def scatter_sums(chunks, rows):
    mine = chunks[0]
    for piece in [shift(chunks[d], "row", rows, d) for d in range(1, rows)]:
        mine = mine + piece
    return mine


def collect(mine, rows):
    return [mine] + [shift(mine, "row", rows, d) for d in range(1, rows)]


def per_device(
    rows,
    cols,
    others,
    ancestor_cov,
    owner_slot,
    parent_pattern,
    parent_factor,
    parent_inverse,
    child_parent,
    child_pattern,
    child_factor,
    child_inverse,
):
    row_slots, col_slots = ancestor_cov.shape[:2]
    up = Layout(*parent_pattern.shape, 0, row_slots, col_slots, rows, cols)
    low = Layout(*child_pattern.shape, 1, row_slots, col_slots, rows, cols)
    flat = lambda x: x.reshape((-1,) + x.shape[2:])
    up_pieces = filled_ring(flat(parent_factor), up.fill, rows) if up.fill else [[ring(flat(parent_factor), rows)]]
    here = jnp.stack([lax.axis_index("row"), lax.axis_index("col")]).astype(jnp.int32)
    index = (here, owner_slot, parent_pattern, child_parent, child_pattern)
    up_tab, up_most = plan(up, index)
    low_tab, low_most = plan(low, index, up, up_tab)
    most = jnp.concatenate([up_most, low_most])
    for axis, size in others:
        seen = most
        for by in range(1, size):
            most = jnp.maximum(most, shift(seen, axis, size, by))
    caps = dict.fromkeys((up.cap_y(a), low.cap_y(b)) for a, b in SPARE)
    caps[(up.full_y, low.full_y)] = None
    branch, over = jnp.int32(0), jnp.bool_(True)
    for up_y, low_y in list(caps)[:-1]:
        over = over & ((most[0] > up_y) | (most[1] > low_y))
        branch = branch + over.astype(jnp.int32)
    gate = [x[-1] for group in up_pieces[:1] for x in group] + [x[-2] for group in up_pieces[2:] for x in group]
    early = [flat(child_factor)]
    early.append(shift(after(early[0], *gate), "row", rows, 1))
    (up_own,) = mult(up, up.full_y, here, up_tab, ancestor_cov, up_pieces)

    def rest(up_y, low_y, args):
        here, ancestors, up_tab, low_tab, up_own, up_pieces, early, inverse, kid_inverse, kid_parent = args
        up_half, low_half = up_y // 2, low_y // 2
        kids = list(early)
        for _ in range(rows - 3):
            kids.append(shift(kids[-1], "row", rows, 1))
        up_other = [swapped(up_own[:up_half], cols)]
        up_parts, _ = terms(up, here, up_tab, up_own, up_pieces)
        kids.append(shift(after(kids[-1], up_other[0], *up_parts), "row", rows, 1))
        up_other.append(swapped(up_own[up_half:up_y], cols))
        ready = after(ancestors, up_other[1])
        halves = (low_half, low_y - low_half)
        low_own, first, second = mult(low, low_y, here, low_tab, ready, [[kids]], up_own, halves)
        up_sum = scatter_sums([after(x, kids[-1]) for x in up_parts], rows)
        theirs = swapped(after(up_sum, low_own), cols)
        low_other = [swapped(after(first, theirs), cols)]
        low_parts, lead = terms(low, here, low_tab, low_own, [[kids]], up_own)
        up_pieces = collect(up_sum + theirs, rows)
        low_sum = scatter_sums(low_parts, rows)
        theirs = swapped(after(low_sum, low_other[0]), cols)
        low_other.append(swapped(after(second, theirs), cols))
        low_pieces = collect(low_sum + theirs, rows)
        parent_cov = spread(up, up_tab, up_own, up_other)
        diag, upper, kid_diag = finish(rows, here, kid_parent, up_pieces, low_pieces, inverse, kid_inverse, lead)
        child_cov = spread(low, low_tab, low_own, low_other)
        return parent_cov, diag, child_cov, upper, kid_diag

    args = (
        here,
        ancestor_cov,
        up_tab,
        low_tab,
        up_own,
        up_pieces,
        early,
        parent_inverse,
        child_inverse,
        child_parent,
    )
    return lax.switch(branch, [functools.partial(rest, *cap) for cap in caps], args)


def solution(mesh):
    in_specs = (
        P(("parts", "row"), "col", None, None),
        P("parts"),
        P(("parts", "sub"), None),
        P(("parts", "sub"), None, "row", None),
        P(("parts", "sub"), None, None),
        P(("parts", "sub")),
        P(("parts", "sub"), None),
        P(("parts", "sub"), None, "row", None),
        P(("parts", "sub"), None, None),
    )
    out_specs = (
        P(("parts", "sub"), "row", None, None),
        P(("parts", "sub"), None, None),
        P(("parts", "sub"), "row", None, None),
        P(("parts", "sub"), None, None),
        P(("parts", "sub"), None, None),
    )
    others = tuple((axis, mesh.shape[axis]) for axis in ("sub", "parts"))
    body = functools.partial(per_device, mesh.shape["row"], mesh.shape["col"], others)
    return jax.shard_map(body, mesh=mesh, in_specs=in_specs, out_specs=out_specs, check_vma=False)
```

```python
import functools

import jax
import jax.numpy as jnp
from jax import lax
from jax.experimental import pallas as pl
from jax.experimental.pallas import tpu as pltpu
from jax.sharding import PartitionSpec as P

VMEM_LIMIT = 50 * 1024 * 1024
FILL = 0
DEPTH = 16
SPARE = ((3, 4), (5, 6))
SMEM = pl.BlockSpec(memory_space=pltpu.SMEM)
VMEM = pl.BlockSpec(memory_space=pltpu.VMEM)
HBM = pl.BlockSpec(memory_space=pl.ANY)
PARAMS = pltpu.CompilerParams(vmem_limit_bytes=VMEM_LIMIT)


def cost(us):
    return pl.CostEstimate(flops=int(us * 1e7), bytes_accessed=int(us * 3.5e4), transcendentals=0)


class Layout:
    def __init__(self, count, length, lead, row_slots, col_slots, rows, cols):
        self.count, self.length, self.lead = count, length, lead
        self.row_slots, self.col_slots, self.rows, self.cols = row_slots, col_slots, rows, cols
        total = count * length
        self.whole = count * (length + lead)
        self.fill = 0 if cols != 2 else min(FILL, self.whole // 2) if lead else self.whole // 2
        self.full_y = count * min(length, row_slots)
        self.mean_y = -(-total // rows)
        products = self.full_y * (min(length, col_slots) + 1)
        self.y_at = 4
        self.out_at = self.y_at + 4 * self.full_y
        self.a_at = self.out_at + count * row_slots
        self.w_at = self.a_at + products
        self.p_at = self.w_at + products
        self.used_at = self.p_at + products
        self.size = self.used_at + total

    def cap_y(self, spare):
        return min(self.full_y, self.mean_y + spare)


def plan_kernel(lay, above, here, owner, parents, kid_parent, kid_pattern, *refs):
    up_tab, refs = (None, refs) if above is None else (refs[0], refs[1:])
    tab, most, row_count, at_block = refs
    row, col = here[0], here[1]
    upper = above is None
    for i in range(lay.rows):
        row_count[i] = 0

    def clear(i, _):
        tab[lay.out_at + i] = -1
        return 0

    lax.fori_loop(0, lay.count * lay.row_slots, clear, 0)
    used, listed, products = jnp.int32(0), jnp.int32(0), jnp.int32(0)
    for m in range(lay.count):
        parent = m if upper else kid_parent[m]
        first_used, first_listed = used, listed

        def place(p, carry):
            used, listed = carry
            slot = owner[parents[parent, p if upper else kid_pattern[m, p]]]
            slot_col, slot_row = slot // lay.col_slots, slot // lay.row_slots
            row_count[slot_row] = row_count[slot_row] + 1
            mine_col, mine_row = slot_col == col, slot_row == row
            at = m * (lay.length + lay.lead) + lay.lead + p

            @pl.when(mine_col)
            def _():
                at_block[used] = slot - col * lay.col_slots
                tab[lay.used_at + used] = at

            @pl.when(mine_row)
            def _():
                local = slot - row * lay.row_slots
                base = lay.y_at + 4 * listed
                tab[base] = m
                tab[base + 1] = local
                tab[base + 2] = at
                tab[base + 3] = 0 if upper else up_tab[above.out_at + parent * lay.row_slots + local]
                tab[lay.out_at + m * lay.row_slots + local] = listed

            return used + mine_col.astype(jnp.int32), listed + mine_row.astype(jnp.int32)

        used, listed = lax.fori_loop(0, lay.length, place, (used, listed))

        def each_row(y, count):
            local = tab[lay.y_at + 4 * y + 1]

            def each_block(w, count):
                tab[lay.a_at + count] = local * lay.col_slots + at_block[w]
                tab[lay.w_at + count] = w
                tab[lay.p_at + count] = y
                return count + 1

            count = lax.fori_loop(first_used, used, each_block, count)
            odd = lax.rem(used - first_used, 2)

            @pl.when(odd == 1)
            def _():
                tab[lay.a_at + count] = local * lay.col_slots
                tab[lay.w_at + count] = lay.count * lay.length
                tab[lay.p_at + count] = y

            return count + odd

        products = lax.fori_loop(first_listed, listed, each_row, products)
    most_row = row_count[0]
    for i in range(1, lay.rows):
        most_row = jnp.maximum(most_row, row_count[i])
    most[0] = most_row
    tab[0] = products
    tab[1] = listed
    tab[2] = used
    tab[3] = 0


def plan(lay, index, above=None, up_tab=None):
    return pl.pallas_call(
        functools.partial(plan_kernel, lay, above),
        out_shape=[jax.ShapeDtypeStruct((lay.size,), jnp.int32), jax.ShapeDtypeStruct((1,), jnp.int32)],
        in_specs=[SMEM] * (5 + (above is not None)),
        out_specs=[SMEM, SMEM],
        scratch_shapes=[pltpu.SMEM((lay.rows,), jnp.int32), pltpu.SMEM((lay.count * lay.length,), jnp.int32)],
        compiler_params=PARAMS,
        cost_estimate=cost(3),
    )(*index, *([] if above is None else [up_tab]))


PLAIN = ((1,), (0,))
TURNED = ((0,), (0,))


def left(x, axis):
    high = x.astype(jnp.bfloat16)
    low = (x - high.astype(jnp.float32)).astype(jnp.bfloat16)
    return jnp.concatenate([high, high, low], axis=axis)


def right(x):
    high = x.astype(jnp.bfloat16)
    low = (x - high.astype(jnp.float32)).astype(jnp.bfloat16)
    return jnp.concatenate([high, low, high], axis=0)


def dot(a, b, dims):
    return lax.dot_general(a, b, (dims, ((), ())), preferred_element_type=jnp.float32)


class Blocks:
    def __init__(self, lay, here, sizes, refs):
        self.row, self.rows = here[0], lay.rows
        if lay.fill:
            own, middle, other = sizes
            first = here[1] == 0
            at = lay.whole - lay.fill
            starts = [jnp.where(first, 0, at), lay.fill, jnp.where(first, at, 0)]
            groups = [own, middle, other]
        else:
            starts, groups = [0], [sizes[0]]
        self.places, self.arrays, i = [], [], 0
        for start, group in zip(starts, groups):
            for size in group:
                self.places.append((start, size))
                self.arrays.append(refs[i : i + lay.rows])
                start = start + size
                i += lay.rows

    def copies(self, at, target, sems, act):
        for (start, size), arrays in zip(self.places, self.arrays):

            @pl.when(jnp.logical_and(at >= start, at < start + size))
            def _():
                for k in range(self.rows):
                    depth = arrays[k].shape[1]
                    owner = lax.rem(self.row - k + self.rows, self.rows)
                    rows = pl.ds(pl.multiple_of(owner * depth, depth), depth)
                    act(pltpu.make_async_copy(arrays[k].at[at - start], target.at[rows, :], sems.at[k]))


def flatten(pieces):
    sizes = tuple(tuple(part[0].shape[0] for part in group) for group in pieces)
    return sizes, [x for group in pieces for part in group for x in part]


def mult_kernel(lay, sizes, parts, here, tab, ancestors, *refs):
    above, refs = (refs[0], refs[1:]) if lay.lead else (None, refs)
    blocks = Blocks(lay, here, sizes, refs[: -6 - parts])
    y, w, wide, slots, w_sems, a_sems = refs[-6 - parts : -5 - parts] + refs[-5:]
    pieces = refs[-5 - parts : -5]
    products, used, listed = tab[0], tab[2], tab[1]
    leads = lay.count * lay.length

    def load(i, act):
        blocks.copies(tab[lay.used_at + i], w.at[i], w_sems.at[i], act)

    def start(copy):
        copy.start()

    def wait(copy):
        copy.wait()

    for m in range(lay.count * lay.lead):
        blocks.copies(jnp.int32(m * (lay.length + lay.lead)), w.at[leads + m], w_sems.at[leads + m], start)

    def begin(i, _):
        load(i, start)
        return 0

    lax.fori_loop(0, used, begin, 0)

    def fetch(i):
        block = tab[lay.a_at + i]
        source = ancestors.at[block // lay.col_slots, block % lay.col_slots]
        return pltpu.make_async_copy(source, slots.at[lax.rem(i, DEPTH)], a_sems.at[lax.rem(i, DEPTH)])

    def fetch_next(i):
        @pl.when(i < products)
        def _():
            fetch(i).start()

    for i in range(DEPTH - 2):
        fetch_next(jnp.int32(i))
    y[...] = jnp.zeros_like(y)
    wide[lay.count * lay.length] = jnp.zeros(wide.shape[1:], jnp.bfloat16)

    if lay.lead:
        for m in range(lay.count):
            blocks.copies(jnp.int32(m * (lay.length + lay.lead)), w.at[leads + m], w_sems.at[leads + m], wait)

        def through(i, _):
            base = lay.y_at + 4 * i
            m, up = tab[base], tab[base + 3]
            y[i] = -dot(left(above[up], 1), right(w[leads + m]), PLAIN)
            return 0

        lax.fori_loop(0, listed, through, 0)

    def spread_out(i, _):
        load(i, wait)
        wide[i] = right(w[i])
        return 0

    lax.fori_loop(0, used, spread_out, 0)

    def step(i, _):
        one, two = 2 * i, 2 * i + 1
        fetch_next(one + DEPTH - 2)
        fetch_next(two + DEPTH - 2)
        fetch(one).wait()
        fetch(two).wait()
        first = dot(left(slots[lax.rem(one, DEPTH)], 1), wide[tab[lay.w_at + one]], PLAIN)
        second = dot(left(slots[lax.rem(two, DEPTH)], 1), wide[tab[lay.w_at + two]], PLAIN)
        y[tab[lay.p_at + one]] += first + second
        return 0

    lax.fori_loop(0, products // 2, step, 0)
    at = 0
    for piece in pieces:
        piece[...] = y[at : at + piece.shape[0]]
        at += piece.shape[0]


def mult(lay, cap_y, here, tab, ancestors, pieces, above=None, parts=()):
    size = ancestors.shape[2]
    sizes, bufs = flatten(pieces)
    held = lay.count * (lay.length + lay.lead)
    return pl.pallas_call(
        functools.partial(mult_kernel, lay, sizes, len(parts)),
        out_shape=[jax.ShapeDtypeStruct((n, size, size), jnp.float32) for n in (cap_y,) + tuple(parts)],
        in_specs=[SMEM, SMEM, HBM] + [VMEM] * lay.lead + [HBM] * len(bufs),
        out_specs=[VMEM] * (1 + len(parts)),
        scratch_shapes=[
            pltpu.VMEM((held, size, size), jnp.float32),
            pltpu.VMEM((lay.count * lay.length + 1, 3 * size, size), jnp.bfloat16),
            pltpu.VMEM((DEPTH, size, size), jnp.float32),
            pltpu.SemaphoreType.DMA((held, lay.rows)),
            pltpu.SemaphoreType.DMA((DEPTH,)),
        ],
        compiler_params=PARAMS,
        cost_estimate=cost(20),
    )(here, tab, ancestors, *([] if above is None else [above]), *bufs)


def put_chunks(row, rows, total, outs):
    depth = outs[0].shape[1]
    for d in range(rows):
        at = lax.rem(row + d, rows)
        outs[d][...] = total[:, pl.ds(pl.multiple_of(at * depth, depth), depth), :]


def chunk_shapes(count, rows, size):
    return [jax.ShapeDtypeStruct((count, size // rows, size), jnp.float32)] * rows


def spread_kernel(lay, tab, own, *refs):
    parts, cov = refs[:-1], refs[-1]
    for m in range(lay.count):
        for s in range(lay.row_slots):
            place = tab[lay.out_at + m * lay.row_slots + s]

            @pl.when(place < 0)
            def _():
                cov[m, s] = jnp.zeros(cov.shape[2:], jnp.float32)

            at = 0
            for part in parts:
                here = jnp.logical_and(place >= at, place < at + part.shape[0])

                @pl.when(here)
                def _():
                    cov[m, s] = -(own[place] + part[place - at])

                at += part.shape[0]


def spread(lay, tab, own, parts):
    size = own.shape[1]
    return pl.pallas_call(
        functools.partial(spread_kernel, lay),
        out_shape=jax.ShapeDtypeStruct((lay.count, lay.row_slots, size, size), jnp.float32),
        in_specs=[SMEM] + [VMEM] * (1 + len(parts)),
        out_specs=VMEM,
        compiler_params=PARAMS,
        cost_estimate=cost(1),
    )(tab, own, *parts)


def terms_kernel(lay, sizes, here, tab, own, *refs):
    above, refs = (refs[0], refs[1:]) if lay.lead else (None, refs)
    w, term, sems = refs[-3:]
    lead, refs = (refs[-4], refs[:-4]) if lay.lead else (None, refs[:-3])
    outs = refs[-lay.rows :]
    blocks = Blocks(lay, here, sizes, refs[: -lay.rows])
    listed = tab[1]

    def load(i, act):
        blocks.copies(tab[lay.y_at + 4 * i + 2], w.at[i], sems.at[i], act)

    def start(copy):
        copy.start()

    def wait(copy):
        copy.wait()

    def begin(i, _):
        load(i, start)
        return 0

    lax.fori_loop(0, listed, begin, 0)
    for m in range(lay.count * lay.lead):
        blocks.copies(jnp.int32(m * (lay.length + lay.lead)), lead.at[m], sems.at[lay.full_y + m], start)
    term[...] = jnp.zeros_like(term)

    def step(y, _):
        load(y, wait)
        base = lay.y_at + 4 * y
        m = tab[base]
        block = w[y]
        term[m] += dot(left(block, 0), right(own[y]), TURNED)
        if lay.lead:
            term[lay.count + m] -= dot(left(above[tab[base + 3]], 0), right(block), TURNED)
        return 0

    lax.fori_loop(0, listed, step, 0)
    for m in range(lay.count * lay.lead):
        blocks.copies(jnp.int32(m * (lay.length + lay.lead)), lead.at[m], sems.at[lay.full_y + m], wait)
    put_chunks(here[0], lay.rows, term, outs)


def terms(lay, here, tab, own, pieces, above=None):
    size = own.shape[1]
    sizes, bufs = flatten(pieces)
    sums = lay.count * (1 + lay.lead)
    outs = chunk_shapes(sums, lay.rows, size) + [jax.ShapeDtypeStruct((lay.count, size, size), jnp.float32)] * lay.lead
    got = pl.pallas_call(
        functools.partial(terms_kernel, lay, sizes),
        out_shape=outs,
        in_specs=[SMEM, SMEM] + [VMEM] * (1 + lay.lead) + [HBM] * len(bufs),
        out_specs=[VMEM] * len(outs),
        scratch_shapes=[
            pltpu.VMEM((lay.full_y, size, size), jnp.float32),
            pltpu.VMEM((sums, size, size), jnp.float32),
            pltpu.SemaphoreType.DMA((lay.full_y + lay.count, lay.rows)),
        ],
        compiler_params=PARAMS,
        cost_estimate=cost(1),
    )(here, tab, own, *([] if above is None else [above]), *bufs)
    return list(got[: lay.rows]), got[-1]


def finish_kernel(rows, count, here, kid_parent, *refs):
    pieces = refs[:rows]
    inverse, kid_inverse, lead, diag, upper, kid_diag, sums, sems = refs[rows:]
    depth = pieces[0].shape[1]
    parents, total = diag.shape[0], pieces[0].shape[0]
    copies = []
    for k in range(rows):
        at = pl.ds(pl.multiple_of(lax.rem(here[0] - k + rows, rows) * depth, depth), depth)
        copies.append(pltpu.make_async_copy(pieces[k].at[pl.ds(0, parents)], diag.at[:, at, :], sems.at[k]))
        copies.append(pltpu.make_async_copy(pieces[k].at[pl.ds(parents, total - parents)], sums.at[:, at, :], sems.at[rows + k]))
    for copy in copies:
        copy.start()
    for copy in copies:
        copy.wait()
    diag[...] = inverse[...] - diag[...]
    for k in range(count):
        v = right(lead[k])
        z = dot(left(diag[kid_parent[k]], 1), v, PLAIN) + sums[count + k]
        upper[k] = -z
        kid_diag[k] = kid_inverse[k] - dot(left(lead[k], 0), right(z), TURNED) - sums[k]


def finish(rows, here, kid_parent, pieces, inverse, kid_inverse, lead):
    return pl.pallas_call(
        functools.partial(finish_kernel, rows, lead.shape[0]),
        out_shape=[
            jax.ShapeDtypeStruct(inverse.shape, jnp.float32),
            jax.ShapeDtypeStruct(kid_inverse.shape, jnp.float32),
            jax.ShapeDtypeStruct(kid_inverse.shape, jnp.float32),
        ],
        in_specs=[SMEM, SMEM] + [HBM] * rows + [VMEM] * 3,
        out_specs=[VMEM] * 3,
        scratch_shapes=[
            pltpu.VMEM((pieces[0].shape[0] - inverse.shape[0],) + lead.shape[1:], jnp.float32),
            pltpu.SemaphoreType.DMA((2 * rows,)),
        ],
        compiler_params=PARAMS,
        cost_estimate=cost(1),
    )(here, kid_parent, *pieces, inverse, kid_inverse, lead)


def shift(x, axis, size, by):
    return lax.ppermute(x, axis, [(i, (i + by) % size) for i in range(size)])


def after(x, *others):
    return lax.optimization_barrier((x,) + others)[0]


def ring(x, rows):
    out = [x]
    for _ in range(rows - 1):
        out.append(shift(out[-1], "row", rows, 1))
    return out


def filled_ring(x, fill, rows):
    first = lax.axis_index("col") == 0
    low, high = x[:fill], x[-fill:]
    mine, theirs = [jnp.where(first, low, high)], [jnp.where(first, high, low)]
    middle = [x[fill:-fill]]
    for step in range(rows - 1):
        send = after(mine[-1], *(theirs[step - 1 : step] if step > 1 else ()))
        mine.append(shift(send, "row", rows, 1))
        if middle[0].shape[0]:
            middle.append(shift(middle[-1], "row", rows, 1))
        if step:
            theirs.append(shift(mine[step], "col", 2, 1))
    theirs.append(shift(mine[-1], "col", 2, 1))
    return [[mine], [middle] if middle[0].shape[0] else [], [theirs]]


def swapped(x, cols):
    if cols == 2:
        return shift(x, "col", 2, 1)
    return lax.psum(x, "col") - x


def scatter_sums(chunks, rows):
    mine = chunks[0]
    for piece in [shift(chunks[d], "row", rows, d) for d in range(1, rows)]:
        mine = mine + piece
    return mine


def collect(mine, rows):
    return [mine] + [shift(mine, "row", rows, d) for d in range(1, rows)]


def per_device(
    rows,
    cols,
    others,
    ancestor_cov,
    owner_slot,
    parent_pattern,
    parent_factor,
    parent_inverse,
    child_parent,
    child_pattern,
    child_factor,
    child_inverse,
):
    row_slots, col_slots = ancestor_cov.shape[:2]
    up = Layout(*parent_pattern.shape, 0, row_slots, col_slots, rows, cols)
    low = Layout(*child_pattern.shape, 1, row_slots, col_slots, rows, cols)
    flat = lambda x: x.reshape((-1,) + x.shape[2:])
    up_pieces = filled_ring(flat(parent_factor), up.fill, rows) if up.fill else [[ring(flat(parent_factor), rows)]]
    here = jnp.stack([lax.axis_index("row"), lax.axis_index("col")]).astype(jnp.int32)
    index = (here, owner_slot, parent_pattern, child_parent, child_pattern)
    up_tab, up_most = plan(up, index)
    low_tab, low_most = plan(low, index, up, up_tab)
    most = jnp.concatenate([up_most, low_most])
    for axis, size in others:
        seen = most
        for by in range(1, size):
            most = jnp.maximum(most, shift(seen, axis, size, by))
    caps = dict.fromkeys((up.cap_y(a), low.cap_y(b)) for a, b in SPARE)
    caps[(up.full_y, low.full_y)] = None
    branch, over = jnp.int32(0), jnp.bool_(True)
    for up_y, low_y in list(caps)[:-1]:
        over = over & ((most[0] > up_y) | (most[1] > low_y))
        branch = branch + over.astype(jnp.int32)
    gate = [x[-1] for group in up_pieces[:1] for x in group] + [x[-2] for group in up_pieces[2:] for x in group]
    early = [flat(child_factor)]
    early.append(shift(after(early[0], *gate), "row", rows, 1))
    (up_own,) = mult(up, up.full_y, here, up_tab, ancestor_cov, up_pieces)

    def rest(up_y, low_y, args):
        here, ancestors, up_tab, low_tab, up_own, up_pieces, early, inverse, kid_inverse, kid_parent = args
        up_half, low_half = up_y // 2, low_y // 2
        kids = list(early)
        for _ in range(rows - 3):
            kids.append(shift(kids[-1], "row", rows, 1))
        up_other = [swapped(up_own[:up_half], cols)]
        up_parts, _ = terms(up, here, up_tab, up_own, up_pieces)
        kids.append(shift(after(kids[-1], up_other[0], *up_parts), "row", rows, 1))
        up_other.append(swapped(up_own[up_half:up_y], cols))
        ready = after(ancestors, up_other[1])
        halves = (low_half, low_y - low_half)
        low_own, first, second = mult(low, low_y, here, low_tab, ready, [[kids]], up_own, halves)
        up_sum = scatter_sums([after(x, kids[-1]) for x in up_parts], rows)
        up_sum, first = lax.optimization_barrier((up_sum, first))
        low_other = [swapped(first, cols)]
        low_parts, lead = terms(low, here, low_tab, low_own, [[kids]], up_own)
        sums = jnp.concatenate([up_sum, scatter_sums(low_parts, rows)])
        theirs = swapped(after(sums, low_other[0]), cols)
        low_other.append(swapped(after(second, theirs), cols))
        pieces = collect(sums + theirs, rows)
        parent_cov = spread(up, up_tab, up_own, up_other)
        child_cov = spread(low, low_tab, low_own, low_other)
        lead = after(lead, child_cov)
        diag, upper, kid_diag = finish(rows, here, kid_parent, pieces, inverse, kid_inverse, lead)
        return parent_cov, diag, child_cov, upper, kid_diag

    args = (
        here,
        ancestor_cov,
        up_tab,
        low_tab,
        up_own,
        up_pieces,
        early,
        parent_inverse,
        child_inverse,
        child_parent,
    )
    return lax.switch(branch, [functools.partial(rest, *cap) for cap in caps], args)


def solution(mesh):
    in_specs = (
        P(("parts", "row"), "col", None, None),
        P("parts"),
        P(("parts", "sub"), None),
        P(("parts", "sub"), None, "row", None),
        P(("parts", "sub"), None, None),
        P(("parts", "sub")),
        P(("parts", "sub"), None),
        P(("parts", "sub"), None, "row", None),
        P(("parts", "sub"), None, None),
    )
    out_specs = (
        P(("parts", "sub"), "row", None, None),
        P(("parts", "sub"), None, None),
        P(("parts", "sub"), "row", None, None),
        P(("parts", "sub"), None, None),
        P(("parts", "sub"), None, None),
    )
    others = tuple((axis, mesh.shape[axis]) for axis in ("sub", "parts"))
    body = functools.partial(per_device, mesh.shape["row"], mesh.shape["col"], others)
    return jax.shard_map(body, mesh=mesh, in_specs=in_specs, out_specs=out_specs, check_vma=False)
```

```python
import functools

import jax
import jax.numpy as jnp
from jax import lax
from jax.experimental import pallas as pl
from jax.experimental.pallas import tpu as pltpu
from jax.sharding import PartitionSpec as P

VMEM_LIMIT = 50 * 1024 * 1024
FILL = 0
DEPTH = 16
SPARE = ((3, 4), (5, 6))
SMEM = pl.BlockSpec(memory_space=pltpu.SMEM)
VMEM = pl.BlockSpec(memory_space=pltpu.VMEM)
HBM = pl.BlockSpec(memory_space=pl.ANY)
PARAMS = pltpu.CompilerParams(vmem_limit_bytes=VMEM_LIMIT)


def cost(us):
    return pl.CostEstimate(flops=int(us * 1e7), bytes_accessed=int(us * 3.5e4), transcendentals=0)


class Layout:
    def __init__(self, count, length, lead, row_slots, col_slots, rows, cols):
        self.count, self.length, self.lead = count, length, lead
        self.row_slots, self.col_slots, self.rows, self.cols = row_slots, col_slots, rows, cols
        total = count * length
        self.whole = count * (length + lead)
        self.fill = 0 if cols != 2 else min(FILL, self.whole // 2) if lead else self.whole // 2
        self.full_y = count * min(length, row_slots)
        self.mean_y = -(-total // rows)
        products = self.full_y * (min(length, col_slots) + 1)
        self.y_at = 4
        self.out_at = self.y_at + 4 * self.full_y
        self.a_at = self.out_at + count * row_slots
        self.w_at = self.a_at + products
        self.p_at = self.w_at + products
        self.used_at = self.p_at + products
        self.size = self.used_at + total

    def cap_y(self, spare):
        return min(self.full_y, self.mean_y + spare)


def plan_kernel(lay, above, here, owner, parents, kid_parent, kid_pattern, *refs):
    up_tab, refs = (None, refs) if above is None else (refs[0], refs[1:])
    tab, most, row_count, at_block = refs
    row, col = here[0], here[1]
    upper = above is None
    for i in range(lay.rows):
        row_count[i] = 0

    def clear(i, _):
        tab[lay.out_at + i] = -1
        return 0

    lax.fori_loop(0, lay.count * lay.row_slots, clear, 0)
    used, listed, products = jnp.int32(0), jnp.int32(0), jnp.int32(0)
    for m in range(lay.count):
        parent = m if upper else kid_parent[m]
        first_used, first_listed = used, listed

        def place(p, carry):
            used, listed = carry
            slot = owner[parents[parent, p if upper else kid_pattern[m, p]]]
            slot_col, slot_row = slot // lay.col_slots, slot // lay.row_slots
            row_count[slot_row] = row_count[slot_row] + 1
            mine_col, mine_row = slot_col == col, slot_row == row
            at = m * (lay.length + lay.lead) + lay.lead + p

            @pl.when(mine_col)
            def _():
                at_block[used] = slot - col * lay.col_slots
                tab[lay.used_at + used] = at

            @pl.when(mine_row)
            def _():
                local = slot - row * lay.row_slots
                base = lay.y_at + 4 * listed
                tab[base] = m
                tab[base + 1] = local
                tab[base + 2] = at
                tab[base + 3] = 0 if upper else up_tab[above.out_at + parent * lay.row_slots + local]
                tab[lay.out_at + m * lay.row_slots + local] = listed

            return used + mine_col.astype(jnp.int32), listed + mine_row.astype(jnp.int32)

        used, listed = lax.fori_loop(0, lay.length, place, (used, listed))

        def each_row(y, count):
            local = tab[lay.y_at + 4 * y + 1]

            def each_block(w, count):
                tab[lay.a_at + count] = local * lay.col_slots + at_block[w]
                tab[lay.w_at + count] = w
                tab[lay.p_at + count] = y
                return count + 1

            count = lax.fori_loop(first_used, used, each_block, count)
            odd = lax.rem(used - first_used, 2)

            @pl.when(odd == 1)
            def _():
                tab[lay.a_at + count] = local * lay.col_slots
                tab[lay.w_at + count] = lay.count * lay.length
                tab[lay.p_at + count] = y

            return count + odd

        products = lax.fori_loop(first_listed, listed, each_row, products)
    most_row = row_count[0]
    for i in range(1, lay.rows):
        most_row = jnp.maximum(most_row, row_count[i])
    most[0] = most_row
    tab[0] = products
    tab[1] = listed
    tab[2] = used
    tab[3] = 0


def plan(lay, index, above=None, up_tab=None):
    return pl.pallas_call(
        functools.partial(plan_kernel, lay, above),
        out_shape=[jax.ShapeDtypeStruct((lay.size,), jnp.int32), jax.ShapeDtypeStruct((1,), jnp.int32)],
        in_specs=[SMEM] * (5 + (above is not None)),
        out_specs=[SMEM, SMEM],
        scratch_shapes=[pltpu.SMEM((lay.rows,), jnp.int32), pltpu.SMEM((lay.count * lay.length,), jnp.int32)],
        compiler_params=PARAMS,
        cost_estimate=cost(3),
    )(*index, *([] if above is None else [up_tab]))


PLAIN = ((1,), (0,))
TURNED = ((0,), (0,))


def left(x, axis):
    high = x.astype(jnp.bfloat16)
    low = (x - high.astype(jnp.float32)).astype(jnp.bfloat16)
    return jnp.concatenate([high, high, low], axis=axis)


def right(x):
    high = x.astype(jnp.bfloat16)
    low = (x - high.astype(jnp.float32)).astype(jnp.bfloat16)
    return jnp.concatenate([high, low, high], axis=0)


def dot(a, b, dims):
    return lax.dot_general(a, b, (dims, ((), ())), preferred_element_type=jnp.float32)


class Blocks:
    def __init__(self, lay, here, sizes, refs):
        self.row, self.rows = here[0], lay.rows
        if lay.fill:
            own, middle, other = sizes
            first = here[1] == 0
            at = lay.whole - lay.fill
            starts = [jnp.where(first, 0, at), lay.fill, jnp.where(first, at, 0)]
            groups = [own, middle, other]
        else:
            starts, groups = [0], [sizes[0]]
        self.places, self.arrays, i = [], [], 0
        for start, group in zip(starts, groups):
            for size in group:
                self.places.append((start, size))
                self.arrays.append(refs[i : i + lay.rows])
                start = start + size
                i += lay.rows

    def copies(self, at, target, sems, act):
        for (start, size), arrays in zip(self.places, self.arrays):

            @pl.when(jnp.logical_and(at >= start, at < start + size))
            def _():
                for k in range(self.rows):
                    depth = arrays[k].shape[1]
                    owner = lax.rem(self.row - k + self.rows, self.rows)
                    rows = pl.ds(pl.multiple_of(owner * depth, depth), depth)
                    act(pltpu.make_async_copy(arrays[k].at[at - start], target.at[rows, :], sems.at[k]))


def flatten(pieces):
    sizes = tuple(tuple(part[0].shape[0] for part in group) for group in pieces)
    return sizes, [x for group in pieces for part in group for x in part]


def mult_kernel(lay, sizes, parts, here, tab, ancestors, *refs):
    above, refs = (refs[0], refs[1:]) if lay.lead else (None, refs)
    blocks = Blocks(lay, here, sizes, refs[: -6 - parts])
    y, w, wide, slots, w_sems, a_sems = refs[-6 - parts : -5 - parts] + refs[-5:]
    pieces = refs[-5 - parts : -5]
    products, used, listed = tab[0], tab[2], tab[1]
    leads = lay.count * lay.length

    def load(i, act):
        blocks.copies(tab[lay.used_at + i], w.at[i], w_sems.at[i], act)

    def start(copy):
        copy.start()

    def wait(copy):
        copy.wait()

    for m in range(lay.count * lay.lead):
        blocks.copies(jnp.int32(m * (lay.length + lay.lead)), w.at[leads + m], w_sems.at[leads + m], start)

    def begin(i, _):
        load(i, start)
        return 0

    lax.fori_loop(0, used, begin, 0)

    def fetch(i):
        block = tab[lay.a_at + i]
        source = ancestors.at[block // lay.col_slots, block % lay.col_slots]
        return pltpu.make_async_copy(source, slots.at[lax.rem(i, DEPTH)], a_sems.at[lax.rem(i, DEPTH)])

    def fetch_next(i):
        @pl.when(i < products)
        def _():
            fetch(i).start()

    for i in range(DEPTH - 2):
        fetch_next(jnp.int32(i))
    y[...] = jnp.zeros_like(y)
    wide[lay.count * lay.length] = jnp.zeros(wide.shape[1:], jnp.bfloat16)

    if lay.lead:
        for m in range(lay.count):
            blocks.copies(jnp.int32(m * (lay.length + lay.lead)), w.at[leads + m], w_sems.at[leads + m], wait)

        def through(i, _):
            base = lay.y_at + 4 * i
            m, up = tab[base], tab[base + 3]
            y[i] = -dot(left(above[up], 1), right(w[leads + m]), PLAIN)
            return 0

        lax.fori_loop(0, listed, through, 0)

    def spread_out(i, _):
        load(i, wait)
        wide[i] = right(w[i])
        return 0

    lax.fori_loop(0, used, spread_out, 0)

    def step(i, _):
        one, two = 2 * i, 2 * i + 1
        fetch_next(one + DEPTH - 2)
        fetch_next(two + DEPTH - 2)
        fetch(one).wait()
        fetch(two).wait()
        first = dot(left(slots[lax.rem(one, DEPTH)], 1), wide[tab[lay.w_at + one]], PLAIN)
        second = dot(left(slots[lax.rem(two, DEPTH)], 1), wide[tab[lay.w_at + two]], PLAIN)
        y[tab[lay.p_at + one]] += first + second
        return 0

    lax.fori_loop(0, products // 2, step, 0)
    at = 0
    for piece in pieces:
        piece[...] = y[at : at + piece.shape[0]]
        at += piece.shape[0]


def mult(lay, cap_y, here, tab, ancestors, pieces, above=None, parts=()):
    size = ancestors.shape[2]
    sizes, bufs = flatten(pieces)
    held = lay.count * (lay.length + lay.lead)
    return pl.pallas_call(
        functools.partial(mult_kernel, lay, sizes, len(parts)),
        out_shape=[jax.ShapeDtypeStruct((n, size, size), jnp.float32) for n in (cap_y,) + tuple(parts)],
        in_specs=[SMEM, SMEM, HBM] + [VMEM] * lay.lead + [HBM] * len(bufs),
        out_specs=[VMEM] * (1 + len(parts)),
        scratch_shapes=[
            pltpu.VMEM((held, size, size), jnp.float32),
            pltpu.VMEM((lay.count * lay.length + 1, 3 * size, size), jnp.bfloat16),
            pltpu.VMEM((DEPTH, size, size), jnp.float32),
            pltpu.SemaphoreType.DMA((held, lay.rows)),
            pltpu.SemaphoreType.DMA((DEPTH,)),
        ],
        compiler_params=PARAMS,
        cost_estimate=cost(20),
    )(here, tab, ancestors, *([] if above is None else [above]), *bufs)


def put_chunks(row, rows, total, outs):
    depth = outs[0].shape[1]
    for d in range(rows):
        at = lax.rem(row + d, rows)
        outs[d][...] = total[:, pl.ds(pl.multiple_of(at * depth, depth), depth), :]


def chunk_shapes(count, rows, size):
    return [jax.ShapeDtypeStruct((count, size // rows, size), jnp.float32)] * rows


def spread_kernel(lay, tab, own, *refs):
    parts, cov = refs[:-1], refs[-1]
    for m in range(lay.count):
        for s in range(lay.row_slots):
            place = tab[lay.out_at + m * lay.row_slots + s]

            @pl.when(place < 0)
            def _():
                cov[m, s] = jnp.zeros(cov.shape[2:], jnp.float32)

            at = 0
            for part in parts:
                here = jnp.logical_and(place >= at, place < at + part.shape[0])

                @pl.when(here)
                def _():
                    cov[m, s] = -(own[place] + part[place - at])

                at += part.shape[0]


def spread(lay, tab, own, parts):
    size = own.shape[1]
    return pl.pallas_call(
        functools.partial(spread_kernel, lay),
        out_shape=jax.ShapeDtypeStruct((lay.count, lay.row_slots, size, size), jnp.float32),
        in_specs=[SMEM] + [VMEM] * (1 + len(parts)),
        out_specs=VMEM,
        compiler_params=PARAMS,
        cost_estimate=cost(1),
    )(tab, own, *parts)


def terms_kernel(lay, sizes, here, tab, own, *refs):
    above, refs = (refs[0], refs[1:]) if lay.lead else (None, refs)
    w, term, sems = refs[-3:]
    lead, refs = (refs[-4], refs[:-4]) if lay.lead else (None, refs[:-3])
    outs = refs[-lay.rows :]
    blocks = Blocks(lay, here, sizes, refs[: -lay.rows])
    listed = tab[1]

    def load(i, act):
        blocks.copies(tab[lay.y_at + 4 * i + 2], w.at[i], sems.at[i], act)

    def start(copy):
        copy.start()

    def wait(copy):
        copy.wait()

    def begin(i, _):
        load(i, start)
        return 0

    lax.fori_loop(0, listed, begin, 0)
    for m in range(lay.count * lay.lead):
        blocks.copies(jnp.int32(m * (lay.length + lay.lead)), lead.at[m], sems.at[lay.full_y + m], start)
    term[...] = jnp.zeros_like(term)

    def step(y, _):
        load(y, wait)
        base = lay.y_at + 4 * y
        m = tab[base]
        block = w[y]
        term[m] += dot(left(block, 0), right(own[y]), TURNED)
        if lay.lead:
            term[lay.count + m] -= dot(left(above[tab[base + 3]], 0), right(block), TURNED)
        return 0

    lax.fori_loop(0, listed, step, 0)
    for m in range(lay.count * lay.lead):
        blocks.copies(jnp.int32(m * (lay.length + lay.lead)), lead.at[m], sems.at[lay.full_y + m], wait)
    put_chunks(here[0], lay.rows, term, outs)


def terms(lay, here, tab, own, pieces, above=None):
    size = own.shape[1]
    sizes, bufs = flatten(pieces)
    sums = lay.count * (1 + lay.lead)
    outs = chunk_shapes(sums, lay.rows, size) + [jax.ShapeDtypeStruct((lay.count, size, size), jnp.float32)] * lay.lead
    got = pl.pallas_call(
        functools.partial(terms_kernel, lay, sizes),
        out_shape=outs,
        in_specs=[SMEM, SMEM] + [VMEM] * (1 + lay.lead) + [HBM] * len(bufs),
        out_specs=[VMEM] * len(outs),
        scratch_shapes=[
            pltpu.VMEM((lay.full_y, size, size), jnp.float32),
            pltpu.VMEM((sums, size, size), jnp.float32),
            pltpu.SemaphoreType.DMA((lay.full_y + lay.count, lay.rows)),
        ],
        compiler_params=PARAMS,
        cost_estimate=cost(1),
    )(here, tab, own, *([] if above is None else [above]), *bufs)
    return list(got[: lay.rows]), got[-1]


def finish_kernel(rows, count, here, kid_parent, *refs):
    pieces = refs[:rows]
    inverse, kid_inverse, lead, diag, upper, kid_diag, sums, sems = refs[rows:]
    depth = pieces[0].shape[1]
    parents, total = diag.shape[0], pieces[0].shape[0]
    copies = []
    for k in range(rows):
        at = pl.ds(pl.multiple_of(lax.rem(here[0] - k + rows, rows) * depth, depth), depth)
        copies.append(pltpu.make_async_copy(pieces[k].at[pl.ds(0, parents)], diag.at[:, at, :], sems.at[k]))
        copies.append(pltpu.make_async_copy(pieces[k].at[pl.ds(parents, total - parents)], sums.at[:, at, :], sems.at[rows + k]))
    for copy in copies:
        copy.start()
    for copy in copies:
        copy.wait()
    diag[...] = inverse[...] - diag[...]
    for k in range(count):
        v = right(lead[k])
        z = dot(left(diag[kid_parent[k]], 1), v, PLAIN) + sums[count + k]
        upper[k] = -z
        kid_diag[k] = kid_inverse[k] - dot(left(lead[k], 0), right(z), TURNED) - sums[k]


def finish(rows, here, kid_parent, pieces, inverse, kid_inverse, lead):
    return pl.pallas_call(
        functools.partial(finish_kernel, rows, lead.shape[0]),
        out_shape=[
            jax.ShapeDtypeStruct(inverse.shape, jnp.float32),
            jax.ShapeDtypeStruct(kid_inverse.shape, jnp.float32),
            jax.ShapeDtypeStruct(kid_inverse.shape, jnp.float32),
        ],
        in_specs=[SMEM, SMEM] + [HBM] * rows + [VMEM] * 3,
        out_specs=[VMEM] * 3,
        scratch_shapes=[
            pltpu.VMEM((pieces[0].shape[0] - inverse.shape[0],) + lead.shape[1:], jnp.float32),
            pltpu.SemaphoreType.DMA((2 * rows,)),
        ],
        compiler_params=PARAMS,
        cost_estimate=cost(1),
    )(here, kid_parent, *pieces, inverse, kid_inverse, lead)


def shift(x, axis, size, by):
    return lax.ppermute(x, axis, [(i, (i + by) % size) for i in range(size)])


def after(x, *others):
    return lax.optimization_barrier((x,) + others)[0]


def ring(x, rows):
    out = [x]
    for _ in range(rows - 1):
        out.append(shift(out[-1], "row", rows, 1))
    return out


def filled_ring(x, fill, rows):
    first = lax.axis_index("col") == 0
    low, high = x[:fill], x[-fill:]
    mine, theirs = [jnp.where(first, low, high)], [jnp.where(first, high, low)]
    middle = [x[fill:-fill]]
    for step in range(rows - 1):
        send = after(mine[-1], *(theirs[step - 1 : step] if step > 1 else ()))
        mine.append(shift(send, "row", rows, 1))
        if middle[0].shape[0]:
            middle.append(shift(middle[-1], "row", rows, 1))
        if step:
            theirs.append(shift(mine[step], "col", 2, 1))
    theirs.append(shift(mine[-1], "col", 2, 1))
    return [[mine], [middle] if middle[0].shape[0] else [], [theirs]]


def swapped(x, cols):
    if cols == 2:
        return shift(x, "col", 2, 1)
    return lax.psum(x, "col") - x


def scatter_sums(chunks, rows):
    mine = chunks[0]
    for piece in [shift(chunks[d], "row", rows, d) for d in range(1, rows)]:
        mine = mine + piece
    return mine


def per_device(
    rows,
    cols,
    others,
    ancestor_cov,
    owner_slot,
    parent_pattern,
    parent_factor,
    parent_inverse,
    child_parent,
    child_pattern,
    child_factor,
    child_inverse,
):
    row_slots, col_slots = ancestor_cov.shape[:2]
    up = Layout(*parent_pattern.shape, 0, row_slots, col_slots, rows, cols)
    low = Layout(*child_pattern.shape, 1, row_slots, col_slots, rows, cols)
    flat = lambda x: x.reshape((-1,) + x.shape[2:])
    up_pieces = filled_ring(flat(parent_factor), up.fill, rows) if up.fill else [[ring(flat(parent_factor), rows)]]
    here = jnp.stack([lax.axis_index("row"), lax.axis_index("col")]).astype(jnp.int32)
    index = (here, owner_slot, parent_pattern, child_parent, child_pattern)
    up_tab, up_most = plan(up, index)
    low_tab, low_most = plan(low, index, up, up_tab)
    most = jnp.concatenate([up_most, low_most])
    for axis, size in others:
        seen = most
        for by in range(1, size):
            most = jnp.maximum(most, shift(seen, axis, size, by))
    caps = dict.fromkeys((up.cap_y(a), low.cap_y(b)) for a, b in SPARE)
    caps[(up.full_y, low.full_y)] = None
    branch, over = jnp.int32(0), jnp.bool_(True)
    for up_y, low_y in list(caps)[:-1]:
        over = over & ((most[0] > up_y) | (most[1] > low_y))
        branch = branch + over.astype(jnp.int32)
    gate = [x[-1] for group in up_pieces[:1] for x in group] + [x[-2] for group in up_pieces[2:] for x in group]
    early = [flat(child_factor)]
    early.append(shift(after(early[0], *gate), "row", rows, 1))
    (up_own,) = mult(up, up.full_y, here, up_tab, ancestor_cov, up_pieces)

    def rest(up_y, low_y, args):
        here, ancestors, up_tab, low_tab, up_own, up_pieces, early, inverse, kid_inverse, kid_parent = args
        up_half, low_half = up_y // 2, low_y // 2
        kids = list(early)
        for _ in range(rows - 3):
            kids.append(shift(kids[-1], "row", rows, 1))
        up_other = [swapped(up_own[:up_half], cols)]
        up_parts, _ = terms(up, here, up_tab, up_own, up_pieces)
        kids.append(shift(after(kids[-1], up_other[0], *up_parts), "row", rows, 1))
        up_other.append(swapped(up_own[up_half:up_y], cols))
        ready = after(ancestors, up_other[1])
        halves = (low_half, low_y - low_half)
        low_own, first, second = mult(low, low_y, here, low_tab, ready, [[kids]], up_own, halves)
        up_sum = scatter_sums([after(x, kids[-1]) for x in up_parts], rows)
        up_sum, first = lax.optimization_barrier((up_sum, first))
        low_other = [swapped(first, cols)]
        low_parts, lead = terms(low, here, low_tab, low_own, [[kids]], up_own)
        sums = jnp.concatenate([up_sum, scatter_sums(low_parts, rows)])
        theirs = swapped(after(sums, low_other[0]), cols)
        low_other.append(swapped(after(second, theirs), cols))
        pieces = ring(sums + theirs, rows)
        parent_cov = spread(up, up_tab, up_own, up_other)
        child_cov = spread(low, low_tab, low_own, low_other)
        lead = after(lead, child_cov)
        diag, upper, kid_diag = finish(rows, here, kid_parent, pieces, inverse, kid_inverse, lead)
        return parent_cov, diag, child_cov, upper, kid_diag

    args = (
        here,
        ancestor_cov,
        up_tab,
        low_tab,
        up_own,
        up_pieces,
        early,
        parent_inverse,
        child_inverse,
        child_parent,
    )
    return lax.switch(branch, [functools.partial(rest, *cap) for cap in caps], args)


def solution(mesh):
    in_specs = (
        P(("parts", "row"), "col", None, None),
        P("parts"),
        P(("parts", "sub"), None),
        P(("parts", "sub"), None, "row", None),
        P(("parts", "sub"), None, None),
        P(("parts", "sub")),
        P(("parts", "sub"), None),
        P(("parts", "sub"), None, "row", None),
        P(("parts", "sub"), None, None),
    )
    out_specs = (
        P(("parts", "sub"), "row", None, None),
        P(("parts", "sub"), None, None),
        P(("parts", "sub"), "row", None, None),
        P(("parts", "sub"), None, None),
        P(("parts", "sub"), None, None),
    )
    others = tuple((axis, mesh.shape[axis]) for axis in ("sub", "parts"))
    body = functools.partial(per_device, mesh.shape["row"], mesh.shape["col"], others)
    return jax.shard_map(body, mesh=mesh, in_specs=in_specs, out_specs=out_specs, check_vma=False)
```

```python
import functools

import jax
import jax.numpy as jnp
from jax import lax
from jax.experimental import pallas as pl
from jax.experimental.pallas import tpu as pltpu
from jax.sharding import PartitionSpec as P

VMEM_LIMIT = 50 * 1024 * 1024
FILL = 0
DEPTH = 16
SPARE = ((3, 4), (5, 6))
SMEM = pl.BlockSpec(memory_space=pltpu.SMEM)
VMEM = pl.BlockSpec(memory_space=pltpu.VMEM)
HBM = pl.BlockSpec(memory_space=pl.ANY)
PARAMS = pltpu.CompilerParams(vmem_limit_bytes=VMEM_LIMIT)


def cost(us):
    return pl.CostEstimate(flops=int(us * 1e7), bytes_accessed=int(us * 3.5e4), transcendentals=0)


class Layout:
    def __init__(self, count, length, lead, row_slots, col_slots, rows, cols):
        self.count, self.length, self.lead = count, length, lead
        self.row_slots, self.col_slots, self.rows, self.cols = row_slots, col_slots, rows, cols
        total = count * length
        self.whole = count * (length + lead)
        self.fill = 0 if cols != 2 else min(FILL, self.whole // 2) if lead else self.whole // 2
        self.full_y = count * min(length, row_slots)
        self.mean_y = -(-total // rows)
        products = self.full_y * (min(length, col_slots) + 1)
        self.y_at = 4
        self.out_at = self.y_at + 4 * self.full_y
        self.a_at = self.out_at + count * row_slots
        self.w_at = self.a_at + products
        self.p_at = self.w_at + products
        self.used_at = self.p_at + products
        self.size = self.used_at + total

    def cap_y(self, spare):
        return min(self.full_y, self.mean_y + spare)


def plan_kernel(lay, above, here, owner, parents, kid_parent, kid_pattern, *refs):
    up_tab, refs = (None, refs) if above is None else (refs[0], refs[1:])
    tab, most, row_count, at_block = refs
    row, col = here[0], here[1]
    upper = above is None
    for i in range(lay.rows):
        row_count[i] = 0

    def clear(i, _):
        tab[lay.out_at + i] = -1
        return 0

    lax.fori_loop(0, lay.count * lay.row_slots, clear, 0)
    used, listed, products = jnp.int32(0), jnp.int32(0), jnp.int32(0)
    for m in range(lay.count):
        parent = m if upper else kid_parent[m]
        first_used, first_listed = used, listed

        def place(p, carry):
            used, listed = carry
            slot = owner[parents[parent, p if upper else kid_pattern[m, p]]]
            slot_col, slot_row = slot // lay.col_slots, slot // lay.row_slots
            row_count[slot_row] = row_count[slot_row] + 1
            mine_col, mine_row = slot_col == col, slot_row == row
            at = m * (lay.length + lay.lead) + lay.lead + p

            @pl.when(mine_col)
            def _():
                at_block[used] = slot - col * lay.col_slots
                tab[lay.used_at + used] = at

            @pl.when(mine_row)
            def _():
                local = slot - row * lay.row_slots
                base = lay.y_at + 4 * listed
                tab[base] = m
                tab[base + 1] = local
                tab[base + 2] = at
                tab[base + 3] = 0 if upper else up_tab[above.out_at + parent * lay.row_slots + local]
                tab[lay.out_at + m * lay.row_slots + local] = listed

            return used + mine_col.astype(jnp.int32), listed + mine_row.astype(jnp.int32)

        used, listed = lax.fori_loop(0, lay.length, place, (used, listed))

        def each_row(y, count):
            local = tab[lay.y_at + 4 * y + 1]

            def each_block(w, count):
                tab[lay.a_at + count] = local * lay.col_slots + at_block[w]
                tab[lay.w_at + count] = w
                tab[lay.p_at + count] = y
                return count + 1

            count = lax.fori_loop(first_used, used, each_block, count)
            odd = lax.rem(used - first_used, 2)

            @pl.when(odd == 1)
            def _():
                tab[lay.a_at + count] = local * lay.col_slots
                tab[lay.w_at + count] = lay.count * lay.length
                tab[lay.p_at + count] = y

            return count + odd

        products = lax.fori_loop(first_listed, listed, each_row, products)
    most_row = row_count[0]
    for i in range(1, lay.rows):
        most_row = jnp.maximum(most_row, row_count[i])
    most[0] = most_row
    tab[0] = products
    tab[1] = listed
    tab[2] = used
    tab[3] = 0


def plan(lay, index, above=None, up_tab=None):
    return pl.pallas_call(
        functools.partial(plan_kernel, lay, above),
        out_shape=[jax.ShapeDtypeStruct((lay.size,), jnp.int32), jax.ShapeDtypeStruct((1,), jnp.int32)],
        in_specs=[SMEM] * (5 + (above is not None)),
        out_specs=[SMEM, SMEM],
        scratch_shapes=[pltpu.SMEM((lay.rows,), jnp.int32), pltpu.SMEM((lay.count * lay.length,), jnp.int32)],
        compiler_params=PARAMS,
        cost_estimate=cost(3),
    )(*index, *([] if above is None else [up_tab]))


PLAIN = ((1,), (0,))


def left(x, axis):
    high = x.astype(jnp.bfloat16)
    low = (x - high.astype(jnp.float32)).astype(jnp.bfloat16)
    return jnp.concatenate([high, high, low], axis=axis)


def right(x):
    high = x.astype(jnp.bfloat16)
    low = (x - high.astype(jnp.float32)).astype(jnp.bfloat16)
    return jnp.concatenate([high, low, high], axis=0)


def dot(a, b, dims):
    return lax.dot_general(a, b, (dims, ((), ())), preferred_element_type=jnp.float32)


class Blocks:
    def __init__(self, lay, here, sizes, refs):
        self.row, self.rows = here[0], lay.rows
        if lay.fill:
            own, middle, other = sizes
            first = here[1] == 0
            at = lay.whole - lay.fill
            starts = [jnp.where(first, 0, at), lay.fill, jnp.where(first, at, 0)]
            groups = [own, middle, other]
        else:
            starts, groups = [0], [sizes[0]]
        self.places, self.arrays, i = [], [], 0
        for start, group in zip(starts, groups):
            for size in group:
                self.places.append((start, size))
                self.arrays.append(refs[i : i + lay.rows])
                start = start + size
                i += lay.rows

    def copies(self, at, target, sems, act):
        for (start, size), arrays in zip(self.places, self.arrays):

            @pl.when(jnp.logical_and(at >= start, at < start + size))
            def _():
                for k in range(self.rows):
                    depth = arrays[k].shape[1]
                    owner = lax.rem(self.row - k + self.rows, self.rows)
                    rows = pl.ds(pl.multiple_of(owner * depth, depth), depth)
                    act(pltpu.make_async_copy(arrays[k].at[at - start], target.at[rows, :], sems.at[k]))


def flatten(pieces):
    sizes = tuple(tuple(part[0].shape[0] for part in group) for group in pieces)
    return sizes, [x for group in pieces for part in group for x in part]


def mult_kernel(lay, sizes, parts, here, tab, ancestors, *refs):
    above, refs = (refs[0], refs[1:]) if lay.lead else (None, refs)
    blocks = Blocks(lay, here, sizes, refs[: -6 - parts])
    y, w, wide, slots, w_sems, a_sems = refs[-6 - parts : -5 - parts] + refs[-5:]
    pieces = refs[-5 - parts : -5]
    products, used, listed = tab[0], tab[2], tab[1]
    leads = lay.count * lay.length

    def load(i, act):
        blocks.copies(tab[lay.used_at + i], w.at[i], w_sems.at[i], act)

    def start(copy):
        copy.start()

    def wait(copy):
        copy.wait()

    for m in range(lay.count * lay.lead):
        blocks.copies(jnp.int32(m * (lay.length + lay.lead)), w.at[leads + m], w_sems.at[leads + m], start)

    def begin(i, _):
        load(i, start)
        return 0

    lax.fori_loop(0, used, begin, 0)

    def fetch(i):
        block = tab[lay.a_at + i]
        source = ancestors.at[block // lay.col_slots, block % lay.col_slots]
        return pltpu.make_async_copy(source, slots.at[lax.rem(i, DEPTH)], a_sems.at[lax.rem(i, DEPTH)])

    def fetch_next(i):
        @pl.when(i < products)
        def _():
            fetch(i).start()

    for i in range(DEPTH - 2):
        fetch_next(jnp.int32(i))
    y[...] = jnp.zeros_like(y)
    wide[lay.count * lay.length] = jnp.zeros(wide.shape[1:], jnp.bfloat16)

    if lay.lead:
        for m in range(lay.count):
            blocks.copies(jnp.int32(m * (lay.length + lay.lead)), w.at[leads + m], w_sems.at[leads + m], wait)

        def through(i, _):
            base = lay.y_at + 4 * i
            m, up = tab[base], tab[base + 3]
            y[i] = -dot(left(above[up], 1), right(w[leads + m]), PLAIN)
            return 0

        lax.fori_loop(0, listed, through, 0)

    def spread_out(i, _):
        load(i, wait)
        wide[i] = right(w[i])
        return 0

    lax.fori_loop(0, used, spread_out, 0)

    def step(i, _):
        one, two = 2 * i, 2 * i + 1
        fetch_next(one + DEPTH - 2)
        fetch_next(two + DEPTH - 2)
        fetch(one).wait()
        fetch(two).wait()
        first = dot(left(slots[lax.rem(one, DEPTH)], 1), wide[tab[lay.w_at + one]], PLAIN)
        second = dot(left(slots[lax.rem(two, DEPTH)], 1), wide[tab[lay.w_at + two]], PLAIN)
        y[tab[lay.p_at + one]] += first + second
        return 0

    lax.fori_loop(0, products // 2, step, 0)
    at = 0
    for piece in pieces:
        piece[...] = y[at : at + piece.shape[0]]
        at += piece.shape[0]


def mult(lay, cap_y, here, tab, ancestors, pieces, above=None, parts=()):
    size = ancestors.shape[2]
    sizes, bufs = flatten(pieces)
    held = lay.count * (lay.length + lay.lead)
    return pl.pallas_call(
        functools.partial(mult_kernel, lay, sizes, len(parts)),
        out_shape=[jax.ShapeDtypeStruct((n, size, size), jnp.float32) for n in (cap_y,) + tuple(parts)],
        in_specs=[SMEM, SMEM, HBM] + [VMEM] * lay.lead + [HBM] * len(bufs),
        out_specs=[VMEM] * (1 + len(parts)),
        scratch_shapes=[
            pltpu.VMEM((held, size, size), jnp.float32),
            pltpu.VMEM((lay.count * lay.length + 1, 3 * size, size), jnp.bfloat16),
            pltpu.VMEM((DEPTH, size, size), jnp.float32),
            pltpu.SemaphoreType.DMA((held, lay.rows)),
            pltpu.SemaphoreType.DMA((DEPTH,)),
        ],
        compiler_params=PARAMS,
        cost_estimate=cost(20),
    )(here, tab, ancestors, *([] if above is None else [above]), *bufs)


def put_chunks(row, rows, total, outs):
    depth = outs[0].shape[1]
    for d in range(rows):
        at = lax.rem(row + d, rows)
        outs[d][...] = total[:, pl.ds(pl.multiple_of(at * depth, depth), depth), :]


def chunk_shapes(count, rows, size):
    return [jax.ShapeDtypeStruct((count, size // rows, size), jnp.float32)] * rows


def spread_kernel(lay, tab, own, *refs):
    parts, cov = refs[:-1], refs[-1]
    for m in range(lay.count):
        for s in range(lay.row_slots):
            place = tab[lay.out_at + m * lay.row_slots + s]

            @pl.when(place < 0)
            def _():
                cov[m, s] = jnp.zeros(cov.shape[2:], jnp.float32)

            at = 0
            for part in parts:
                here = jnp.logical_and(place >= at, place < at + part.shape[0])

                @pl.when(here)
                def _():
                    cov[m, s] = -(own[place] + part[place - at])

                at += part.shape[0]


def spread(lay, tab, own, parts):
    size = own.shape[1]
    return pl.pallas_call(
        functools.partial(spread_kernel, lay),
        out_shape=jax.ShapeDtypeStruct((lay.count, lay.row_slots, size, size), jnp.float32),
        in_specs=[SMEM] + [VMEM] * (1 + len(parts)),
        out_specs=VMEM,
        compiler_params=PARAMS,
        cost_estimate=cost(1),
    )(tab, own, *parts)


def terms_kernel(lay, sizes, here, tab, own, *refs):
    above, refs = (refs[0], refs[1:]) if lay.lead else (None, refs)
    w, term, sems = refs[-3:]
    lead, refs = (refs[-4], refs[:-4]) if lay.lead else (None, refs[:-3])
    outs = refs[-lay.rows :]
    blocks = Blocks(lay, here, sizes, refs[: -lay.rows])
    listed = tab[1]

    def load(i, act):
        blocks.copies(tab[lay.y_at + 4 * i + 2], w.at[i], sems.at[i], act)

    def start(copy):
        copy.start()

    def wait(copy):
        copy.wait()

    def begin(i, _):
        load(i, start)
        return 0

    lax.fori_loop(0, listed, begin, 0)
    for m in range(lay.count * lay.lead):
        blocks.copies(jnp.int32(m * (lay.length + lay.lead)), lead.at[m], sems.at[lay.full_y + m], start)
    term[...] = jnp.zeros_like(term)

    def step(y, _):
        load(y, wait)
        base = lay.y_at + 4 * y
        m = tab[base]
        block = w[y]
        term[m] += dot(left(block.T, 1), right(own[y]), PLAIN)
        if lay.lead:
            term[lay.count + m] -= dot(left(above[tab[base + 3]].T, 1), right(block), PLAIN)
        return 0

    lax.fori_loop(0, listed, step, 0)
    for m in range(lay.count * lay.lead):
        blocks.copies(jnp.int32(m * (lay.length + lay.lead)), lead.at[m], sems.at[lay.full_y + m], wait)
    put_chunks(here[0], lay.rows, term, outs)


def terms(lay, here, tab, own, pieces, above=None):
    size = own.shape[1]
    sizes, bufs = flatten(pieces)
    sums = lay.count * (1 + lay.lead)
    outs = chunk_shapes(sums, lay.rows, size) + [jax.ShapeDtypeStruct((lay.count, size, size), jnp.float32)] * lay.lead
    got = pl.pallas_call(
        functools.partial(terms_kernel, lay, sizes),
        out_shape=outs,
        in_specs=[SMEM, SMEM] + [VMEM] * (1 + lay.lead) + [HBM] * len(bufs),
        out_specs=[VMEM] * len(outs),
        scratch_shapes=[
            pltpu.VMEM((lay.full_y, size, size), jnp.float32),
            pltpu.VMEM((sums, size, size), jnp.float32),
            pltpu.SemaphoreType.DMA((lay.full_y + lay.count, lay.rows)),
        ],
        compiler_params=PARAMS,
        cost_estimate=cost(1),
    )(here, tab, own, *([] if above is None else [above]), *bufs)
    return list(got[: lay.rows]), got[-1]


def finish_kernel(rows, count, here, kid_parent, *refs):
    pieces = refs[:rows]
    inverse, kid_inverse, lead, diag, upper, kid_diag, sums, sems = refs[rows:]
    depth = pieces[0].shape[1]
    parents, total = diag.shape[0], pieces[0].shape[0]
    copies = []
    for k in range(rows):
        at = pl.ds(pl.multiple_of(lax.rem(here[0] - k + rows, rows) * depth, depth), depth)
        copies.append(pltpu.make_async_copy(pieces[k].at[pl.ds(0, parents)], diag.at[:, at, :], sems.at[k]))
        copies.append(pltpu.make_async_copy(pieces[k].at[pl.ds(parents, total - parents)], sums.at[:, at, :], sems.at[rows + k]))
    for copy in copies:
        copy.start()
    for copy in copies:
        copy.wait()
    diag[...] = inverse[...] - diag[...]
    for k in range(count):
        v = right(lead[k])
        z = dot(left(diag[kid_parent[k]], 1), v, PLAIN) + sums[count + k]
        upper[k] = -z
        kid_diag[k] = kid_inverse[k] - dot(left(lead[k].T, 1), right(z), PLAIN) - sums[k]


def finish(rows, here, kid_parent, pieces, inverse, kid_inverse, lead):
    return pl.pallas_call(
        functools.partial(finish_kernel, rows, lead.shape[0]),
        out_shape=[
            jax.ShapeDtypeStruct(inverse.shape, jnp.float32),
            jax.ShapeDtypeStruct(kid_inverse.shape, jnp.float32),
            jax.ShapeDtypeStruct(kid_inverse.shape, jnp.float32),
        ],
        in_specs=[SMEM, SMEM] + [HBM] * rows + [VMEM] * 3,
        out_specs=[VMEM] * 3,
        scratch_shapes=[
            pltpu.VMEM((pieces[0].shape[0] - inverse.shape[0],) + lead.shape[1:], jnp.float32),
            pltpu.SemaphoreType.DMA((2 * rows,)),
        ],
        compiler_params=PARAMS,
        cost_estimate=cost(1),
    )(here, kid_parent, *pieces, inverse, kid_inverse, lead)


def shift(x, axis, size, by):
    return lax.ppermute(x, axis, [(i, (i + by) % size) for i in range(size)])


def after(x, *others):
    return lax.optimization_barrier((x,) + others)[0]


def ring(x, rows):
    out = [x]
    for _ in range(rows - 1):
        out.append(shift(out[-1], "row", rows, 1))
    return out


def filled_ring(x, fill, rows):
    first = lax.axis_index("col") == 0
    low, high = x[:fill], x[-fill:]
    mine, theirs = [jnp.where(first, low, high)], [jnp.where(first, high, low)]
    middle = [x[fill:-fill]]
    for step in range(rows - 1):
        send = after(mine[-1], *(theirs[step - 1 : step] if step > 1 else ()))
        mine.append(shift(send, "row", rows, 1))
        if middle[0].shape[0]:
            middle.append(shift(middle[-1], "row", rows, 1))
        if step:
            theirs.append(shift(mine[step], "col", 2, 1))
    theirs.append(shift(mine[-1], "col", 2, 1))
    return [[mine], [middle] if middle[0].shape[0] else [], [theirs]]


def swapped(x, cols):
    if cols == 2:
        return shift(x, "col", 2, 1)
    return lax.psum(x, "col") - x


def scatter_sums(chunks, rows):
    mine = chunks[0]
    for piece in [shift(chunks[d], "row", rows, d) for d in range(1, rows)]:
        mine = mine + piece
    return mine


def per_device(
    rows,
    cols,
    others,
    ancestor_cov,
    owner_slot,
    parent_pattern,
    parent_factor,
    parent_inverse,
    child_parent,
    child_pattern,
    child_factor,
    child_inverse,
):
    row_slots, col_slots = ancestor_cov.shape[:2]
    up = Layout(*parent_pattern.shape, 0, row_slots, col_slots, rows, cols)
    low = Layout(*child_pattern.shape, 1, row_slots, col_slots, rows, cols)
    flat = lambda x: x.reshape((-1,) + x.shape[2:])
    up_pieces = filled_ring(flat(parent_factor), up.fill, rows) if up.fill else [[ring(flat(parent_factor), rows)]]
    here = jnp.stack([lax.axis_index("row"), lax.axis_index("col")]).astype(jnp.int32)
    index = (here, owner_slot, parent_pattern, child_parent, child_pattern)
    up_tab, up_most = plan(up, index)
    low_tab, low_most = plan(low, index, up, up_tab)
    most = jnp.concatenate([up_most, low_most])
    for axis, size in others:
        seen = most
        for by in range(1, size):
            most = jnp.maximum(most, shift(seen, axis, size, by))
    caps = dict.fromkeys((up.cap_y(a), low.cap_y(b)) for a, b in SPARE)
    caps[(up.full_y, low.full_y)] = None
    branch, over = jnp.int32(0), jnp.bool_(True)
    for up_y, low_y in list(caps)[:-1]:
        over = over & ((most[0] > up_y) | (most[1] > low_y))
        branch = branch + over.astype(jnp.int32)
    gate = [x[-1] for group in up_pieces[:1] for x in group] + [x[-2] for group in up_pieces[2:] for x in group]
    early = [flat(child_factor)]
    early.append(shift(after(early[0], *gate), "row", rows, 1))
    (up_own,) = mult(up, up.full_y, here, up_tab, ancestor_cov, up_pieces)

    def rest(up_y, low_y, args):
        here, ancestors, up_tab, low_tab, up_own, up_pieces, early, inverse, kid_inverse, kid_parent = args
        up_half, low_half = up_y // 2, low_y // 2
        kids = list(early)
        for _ in range(rows - 3):
            kids.append(shift(kids[-1], "row", rows, 1))
        up_other = [swapped(up_own[:up_half], cols)]
        up_parts, _ = terms(up, here, up_tab, up_own, up_pieces)
        kids.append(shift(after(kids[-1], up_other[0], *up_parts), "row", rows, 1))
        up_other.append(swapped(up_own[up_half:up_y], cols))
        ready = after(ancestors, up_other[1])
        halves = (low_half, low_y - low_half)
        low_own, first, second = mult(low, low_y, here, low_tab, ready, [[kids]], up_own, halves)
        up_sum = scatter_sums([after(x, kids[-1]) for x in up_parts], rows)
        up_sum, first = lax.optimization_barrier((up_sum, first))
        low_other = [swapped(first, cols)]
        low_parts, lead = terms(low, here, low_tab, low_own, [[kids]], up_own)
        sums = jnp.concatenate([up_sum, scatter_sums(low_parts, rows)])
        theirs = swapped(after(sums, low_other[0]), cols)
        low_other.append(swapped(after(second, theirs), cols))
        pieces = ring(sums + theirs, rows)
        parent_cov = spread(up, up_tab, up_own, up_other)
        child_cov = spread(low, low_tab, low_own, low_other)
        lead = after(lead, child_cov)
        diag, upper, kid_diag = finish(rows, here, kid_parent, pieces, inverse, kid_inverse, lead)
        return parent_cov, diag, child_cov, upper, kid_diag

    args = (
        here,
        ancestor_cov,
        up_tab,
        low_tab,
        up_own,
        up_pieces,
        early,
        parent_inverse,
        child_inverse,
        child_parent,
    )
    return lax.switch(branch, [functools.partial(rest, *cap) for cap in caps], args)


def solution(mesh):
    in_specs = (
        P(("parts", "row"), "col", None, None),
        P("parts"),
        P(("parts", "sub"), None),
        P(("parts", "sub"), None, "row", None),
        P(("parts", "sub"), None, None),
        P(("parts", "sub")),
        P(("parts", "sub"), None),
        P(("parts", "sub"), None, "row", None),
        P(("parts", "sub"), None, None),
    )
    out_specs = (
        P(("parts", "sub"), "row", None, None),
        P(("parts", "sub"), None, None),
        P(("parts", "sub"), "row", None, None),
        P(("parts", "sub"), None, None),
        P(("parts", "sub"), None, None),
    )
    others = tuple((axis, mesh.shape[axis]) for axis in ("sub", "parts"))
    body = functools.partial(per_device, mesh.shape["row"], mesh.shape["col"], others)
    return jax.shard_map(body, mesh=mesh, in_specs=in_specs, out_specs=out_specs, check_vma=False)
```
